512 devices in a mesh: vec: 32 (over x_lo, z), lat: 16 (over x_hi, y, core).
Axes of the slice: x: 4 (x_hi: 2, x_lo: 2; x = x_hi * 2 + x_lo), y: 4, z: 16, core: 2. Of those that a mesh axis runs over, the one named last changes fastest.
Arguments:
- perturb: float32 [128, 8, 384, 720], P('vec', None, 'lat'), may hold values from -6 to 6
- trajectory: bfloat16 [32, 3, 8, 384, 720], P('vec', None, None, 'lat'), may hold values from -3 to 3
- hour_slot: int32 [2], replicated, may hold values from 0 to 31, as said below
- sea_mask: int32 [384, 720], P('lat'), may hold values 0 or 1
Outputs:
- evolved: float32 [128, 8, 384, 720], P('vec', None, 'lat')
The draws below stay inside these ranges and needn't reach their ends.
Inputs may be any that keep to these rules, and one draw needn't show every extreme that they name: `hour_slot`: 2 distinct indices of saved hours; one of them is always the last saved hour, 31.
All inputs are finite; a program needn't handle non-finite values. No bound on the sum of `sea_mask` on one device may be relied on, other than what follows from the above.
Results may differ from the reference program's by a relative error of at most 0.0003.
Values may be sent and summed in bfloat16 or wider, within the bound.
No kernel may reach another device: no remote copies, remote signals or barrier semaphores. Data moves between devices by JAX's collectives and lax.ppermute only.
A program may use at most 128 MiB of HBM per device.

```python
import jax
import jax.numpy as jnp
from jax import lax

LON = 720
LEV = 8
HOURS = 2
SLOTS = 1
NLAT = 384
VECS = 128
STORED = 32
N_VEC = 32


def draw_hour_slot(key, part):
    key = jax.random.fold_in(key, 11)
    key_rest = jax.random.fold_in(key, 1)
    key_place = jax.random.fold_in(key, 2)
    last_slot = N_VEC * SLOTS - 1
    others = jax.random.permutation(key_rest, last_slot)[:HOURS].astype(jnp.int32)
    place = jax.random.randint(key_place, (), 0, HOURS).astype(jnp.int32)
    positions = jnp.arange(HOURS, dtype=jnp.int32)
    picked = jnp.clip(positions - (positions > place).astype(jnp.int32), 0, HOURS - 1)
    return jnp.where(positions == place, last_slot, others[picked]).astype(jnp.int32)


def with_ends(entries, stream_key, least, high):
    dims = entries.shape
    spot = [jax.random.randint(jax.random.fold_in(stream_key, axis), (), 0, dims[axis]) for axis in range(len(dims))]
    entries = entries.at[tuple(spot)].set(least)
    longest = dims.index(max(dims))
    spot[longest] = (spot[longest] + 1) % dims[longest]
    return entries.at[tuple(spot)].set(high)


def level_of(stream_key, extent, pieces, smallest, largest):
    loudness, own = 1.0, jax.random.fold_in(stream_key, 6)
    for position, parts in pieces:
        steps = jnp.exp(jax.random.uniform(jax.random.fold_in(own, position), (parts,), jnp.float32, smallest / len(pieces), largest / len(pieces)))
        loudness = loudness * jnp.repeat(steps, extent[position] // parts).reshape([-1 if axis == position else 1 for axis in range(len(extent))])
    return loudness


def centred(stream_key, extent, scale, reach, cuts=(), kind=jnp.bfloat16):
    factor_of = level_of(stream_key, extent, cuts, -0.22, 0.18) if cuts else 1.0
    drawn = jax.random.normal(stream_key, extent, jnp.float32) * scale * factor_of
    return jnp.minimum(jnp.maximum(drawn, -reach), reach).astype(kind)


def setup_inputs(seed: int = 0) -> dict:
    key_of = jax.random.split(jax.random.key(seed), 5)
    perturb = centred(key_of[0], (VECS, LEV, NLAT, LON), 1.0, 6.0, ((0, 32), (2, 16)), jnp.float32)
    trajectory = centred(key_of[1], (STORED, 3, LEV, NLAT, LON), 1.0, 3.0, ((0, 32), (3, 16)))
    hour_slot = draw_hour_slot(jax.random.fold_in(key_of[4], 71), 0)
    sea_mask = with_ends((jax.random.randint(key_of[3], (NLAT, LON), 0, 10) < 7).astype(jnp.int32), jax.random.fold_in(key_of[3], 1), 0, 1)
    return {"perturb": perturb, "trajectory": trajectory, "hour_slot": hour_slot, "sea_mask": sea_mask}


def update_rows(padded, fields, ocean_mask):
    center = padded[:, :, 1:-1]
    northern = padded[:, :, 2:]
    southern = padded[:, :, :-2]
    eastern = jnp.roll(center, -1, axis=3)
    western = jnp.roll(center, 1, axis=3)
    upper_level = jnp.concatenate([center[:, :1], center[:, :-1]], axis=1)
    lower_level = jnp.concatenate([center[:, 1:], center[:, -1:]], axis=1)
    diffuse = 0.06 + 0.015 * fields[0]
    zonal_speed = 0.15 * fields[1]
    merid_speed = 0.15 * fields[2]
    change = diffuse * (eastern + western + northern + southern - 4.0 * center)
    change = change - zonal_speed * (eastern - western) - merid_speed * (northern - southern)
    change = change + 0.1 * (upper_level + lower_level - 2.0 * center)
    return ocean_mask * (center + change)


def reference(perturb, trajectory, hour_slot, sea_mask):
    ocean_mask = sea_mask.astype(jnp.float32)
    tracer = perturb
    for hour_step in range(HOURS):
        fields = lax.dynamic_index_in_dim(trajectory, hour_slot[hour_step], 0, keepdims=False).astype(jnp.float32)
        padded = jnp.pad(tracer, ((0, 0), (0, 0), (1, 1), (0, 0)))
        tracer = update_rows(padded, fields, ocean_mask)
    return tracer
```

```python
import jax
import jax.numpy as jnp
from jax import lax
from jax.experimental import pallas as pl
from jax.experimental.pallas import tpu as pltpu
from jax.sharding import PartitionSpec as P

LAST = 31
RING = 16
ROWS = 8


def lanes_next(x):
    return jnp.concatenate([x[..., 1:], x[..., :1]], axis=-1)


def lanes_prev(x):
    return jnp.concatenate([x[..., -1:], x[..., :-1]], axis=-1)


def advance(c, n, s, u, b, f0, f1, f2, mask):
    e, w = lanes_next(c), lanes_prev(c)
    diffuse = 0.06 + 0.015 * f0
    change = diffuse * (e + w + n + s - 4.0 * c)
    change = change - (0.15 * f1) * (e - w) - (0.15 * f2) * (n - s)
    change = change + 0.1 * (u + b - 2.0 * c)
    return mask * (c + change)


def steps_kernel(
    flag_ref, q_ref, south_ref, north_ref, mask_ref, mask_s_ref, mask_n_ref,
    edge_s_ref, edge_n_ref, *refs,
):
    chunks = len(refs[:-5]) // 2
    v_refs, w_refs = refs[:chunks], refs[chunks : 2 * chunks]
    out_ref, mid_ref, mid_s_ref, mid_n_ref, field_ref = refs[-5:]
    vecs, levs, rows, lon = q_ref.shape
    first_v = flag_ref[0] == 1
    row = lax.broadcasted_iota(jnp.int32, (rows, lon), 0)
    mask = mask_ref[...].astype(jnp.float32)

    def fields_of(level, hour):
        use_v = first_v if hour == 0 else jnp.logical_not(first_v)

        @pl.when(use_v)
        def _():
            for c in range(chunks):
                for k in range(3):
                    field_ref[k, c * ROWS : (c + 1) * ROWS] = v_refs[c][k, level].astype(jnp.float32)

        @pl.when(jnp.logical_not(use_v))
        def _():
            for c in range(chunks):
                for k in range(3):
                    field_ref[k, c * ROWS : (c + 1) * ROWS] = w_refs[c][k, level].astype(jnp.float32)

        return field_ref[0], field_ref[1], field_ref[2]

    def hour_of(src_ref, dst_ref, halo_s, halo_n, hour):
        def level_step(level, carry):
            f0, f1, f2 = fields_of(level, hour)
            up = jnp.maximum(level - 1, 0)
            low = jnp.minimum(level + 1, levs - 1)
            for v in range(vecs):
                c = src_ref[v, level]
                n = jnp.where(row == rows - 1, halo_n(v, level), pltpu.roll(c, rows - 1, 0))
                s = jnp.where(row == 0, halo_s(v, level), pltpu.roll(c, 1, 0))
                dst_ref[v, level] = advance(
                    c, n, s, src_ref[v, up], src_ref[v, low], f0, f1, f2, mask
                )
            return carry

        lax.fori_loop(0, levs, level_step, 0)

    lev = lax.broadcasted_iota(jnp.int32, (levs, lon), 0)

    def edge_rows(c, n, s, edge_ref, edge_mask_ref):
        u = jnp.where(lev == 0, c, pltpu.roll(c, 1, 0))
        b = jnp.where(lev == levs - 1, c, pltpu.roll(c, levs - 1, 0))
        f = [edge_ref[k].astype(jnp.float32) for k in range(3)]
        return advance(c, n, s, u, b, *f, edge_mask_ref[...].astype(jnp.float32))

    for v in range(vecs):
        first = jnp.concatenate([q_ref[v, z, 0:1] for z in range(levs)], axis=0)
        last = jnp.concatenate([q_ref[v, z, rows - 1 : rows] for z in range(levs)], axis=0)
        mid_s_ref[v] = edge_rows(south_ref[1, v], first, south_ref[0, v], edge_s_ref, mask_s_ref)
        mid_n_ref[v] = edge_rows(north_ref[0, v], north_ref[1, v], last, edge_n_ref, mask_n_ref)

    hour_of(
        q_ref, mid_ref,
        lambda v, z: south_ref[1, v, pl.ds(z, 1)],
        lambda v, z: north_ref[0, v, pl.ds(z, 1)],
        0,
    )
    hour_of(
        mid_ref, out_ref,
        lambda v, z: mid_s_ref[v, pl.ds(z, 1)],
        lambda v, z: mid_n_ref[v, pl.ds(z, 1)],
        1,
    )


def two_hours(flag, q, south, north, mask, mask_s, mask_n, edge_s, edge_n, vs, ws):
    vecs, levs, rows, lon = q.shape
    vmem = pl.BlockSpec(memory_space=pltpu.VMEM)
    args = [q, south, north, mask, mask_s, mask_n, edge_s, edge_n, *vs, *ws]
    return pl.pallas_call(
        steps_kernel,
        out_shape=jax.ShapeDtypeStruct(q.shape, jnp.float32),
        in_specs=[pl.BlockSpec(memory_space=pltpu.SMEM)] + [vmem] * len(args),
        out_specs=vmem,
        scratch_shapes=[
            pltpu.VMEM(q.shape, jnp.float32),
            pltpu.VMEM((vecs, levs, lon), jnp.float32),
            pltpu.VMEM((vecs, levs, lon), jnp.float32),
            pltpu.VMEM((3, rows, lon), jnp.float32),
        ],
        compiler_params=pltpu.CompilerParams(vmem_limit_bytes=40 * 1024 * 1024),
        name="two_hours",
    )(flag, *args)


TREE = (
    (((0, 4),), ((0, -4),)),
    (((4, 6), (-4, -6)), ((4, 2), (-4, -2))),
    (
        ((6, 7), (-6, -7), (2, 3), (-2, -3)),
        ((6, 5), (-6, -5), (2, 1), (-2, -1)),
        ((6, 8),),
    ),
)


def spread_from(other, hop, swap_edges):
    roots = (other % RING, LAST % RING)

    def pairs(moves):
        return [
            (x * RING + (roots[x] + a) % RING, x * RING + (roots[x] + b) % RING)
            for x in range(2)
            for a, b in moves
        ]

    swap = [(i, (i + RING) % (2 * RING)) for i in range(2 * RING)]

    def run(*chunks):
        vs, ws, tie = [], [], None
        for own in chunks:
            value = own if tie is None else own + tie
            if other >= RING:
                crossed = lax.ppermute(value, "vec", [(other, other - RING)])
                value = jnp.where(lax.axis_index("vec") == other - RING, crossed, value)
            for depth, level in enumerate(TREE):
                got = [lax.ppermute(value, "vec", pairs(moves)) for moves in level]
                if depth == 0:
                    tie = (got[0][0, 0, 0, 0] + got[1][0, 0, 0, 0]) * 0
                total = got[0]
                for more in got[1:]:
                    total = total + more
                value = jnp.where(hop <= depth, value, total)
            vs.append(value)
            ws.append(lax.ppermute(value, "vec", swap))
        return (*vs, *ws)

    return run


def shards(perturb, trajectory, hour_slot, sea_mask):
    lat = lax.axis_size("lat")
    me = lax.axis_index("vec")
    column, z = me // RING, me % RING
    other = hour_slot[0] + hour_slot[1] - LAST
    root = jnp.where(column == 1, LAST % RING, other % RING)
    away = (z - root) % RING
    away = jnp.minimum(away, RING - away)
    hop = jnp.where(away == 0, 0, jnp.where(away == 4, 1, jnp.where((away == 2) | (away == 6), 2, 3)))
    first_v = (hour_slot[0] == LAST) == (column == 1)

    northward = [(i, i + 1) for i in range(lat - 1)]
    southward = [(i + 1, i) for i in range(lat - 1)]

    def edge(rows):
        return jnp.moveaxis(rows, -2, 0)

    south = lax.ppermute(edge(perturb[:, :, -2:]), "lat", northward)
    north = lax.ppermute(edge(perturb[:, :, :2]), "lat", southward)
    ocean = sea_mask.astype(jnp.float32)
    mask_s = lax.ppermute(ocean[-1:], "lat", northward)
    mask_n = lax.ppermute(ocean[:1], "lat", southward)

    field = trajectory[0]
    rows = field.shape[2]
    chunks = [field[:, :, r : r + ROWS] for r in range(0, rows, ROWS)]
    spread = lax.switch(
        other,
        [spread_from(slot, hop, None) for slot in range(LAST)],
        *chunks,
    )
    vs, ws = spread[: len(chunks)], spread[len(chunks) :]
    lower = jnp.where(first_v, vs[0][:, :, 0], ws[0][:, :, 0])
    upper = jnp.where(first_v, vs[-1][:, :, -1], ws[-1][:, :, -1])
    edge_s = lax.ppermute(upper, "lat", northward)
    edge_n = lax.ppermute(lower, "lat", southward)
    return two_hours(
        first_v.astype(jnp.int32)[None],
        perturb, south, north, sea_mask, mask_s, mask_n, edge_s, edge_n, vs, ws,
    )


def solution(mesh):
    return jax.shard_map(
        shards,
        mesh=mesh,
        in_specs=(
            P("vec", None, "lat", None),
            P("vec", None, None, "lat", None),
            P(),
            P("lat", None),
        ),
        out_specs=P("vec", None, "lat", None),
        check_vma=False,
    )
```

```python
import jax
import jax.numpy as jnp
from jax import lax
from jax.experimental import pallas as pl
from jax.experimental.pallas import tpu as pltpu
from jax.sharding import PartitionSpec as P

COLUMNS = 2
RING = 16
LANES = 128
FIELDS = 3
CUT = 40
PIECE = 112
VMEM_LIMIT = 48 * 1024 * 1024


def tile_parts(rows, half):
    total = FIELDS * rows
    base = 3 * half
    return (
        (base, 0, total, 0, 0),
        (base + 1, 0, CUT, 0, total),
        (base + 1, CUT, total, 1, 0),
        (base + 2, 0, total, 1, total - CUT),
    )


def field_parts(rows, half):
    parts = []
    for tile, start, stop, column, at in tile_parts(rows, half):
        for k in range(FIELDS):
            lo, hi = max(start, k * rows), min(stop, (k + 1) * rows)
            if lo < hi:
                parts.append((k, tile, lo - k * rows, hi - k * rows, column, at + lo - start))
    return parts


def pack_kernel(field_ref, piece_ref):
    _, levs, rows, lon = field_ref.shape[1:]
    for level in range(levs):
        for half in range(2):
            for k, tile, lo, hi, column, at in field_parts(rows, half):
                p = column * RING + level * 2 + half
                left, right = tile * LANES, min((tile + 1) * LANES, lon)
                piece_ref[p, at : at + hi - lo, : right - left] = field_ref[0, k, level, lo:hi, left:right]


def pack(trajectory):
    return pl.pallas_call(
        pack_kernel,
        out_shape=jax.ShapeDtypeStruct((COLUMNS * RING, PIECE, LANES), trajectory.dtype),
        in_specs=[pl.BlockSpec(memory_space=pltpu.VMEM)],
        out_specs=pl.BlockSpec(memory_space=pltpu.VMEM),
        compiler_params=pltpu.CompilerParams(vmem_limit_bytes=VMEM_LIMIT),
        name="pack",
    )(trajectory)


def lanes_next(x):
    return jnp.concatenate([x[..., 1:], x[..., :1]], axis=-1)


def lanes_prev(x):
    return jnp.concatenate([x[..., -1:], x[..., :-1]], axis=-1)


def advance(c, n, s, u, b, f0, f1, f2, mask):
    e, w = lanes_next(c), lanes_prev(c)
    diffuse = 0.06 + 0.015 * f0
    change = diffuse * (e + w + n + s - 4.0 * c)
    change = change - (0.15 * f1) * (e - w) - (0.15 * f2) * (n - s)
    change = change + 0.1 * (u + b - 2.0 * c)
    return mask * (c + change)


def hour_kernel(
    column_ref, q_ref, south_ref, north_ref, mask_ref, own_ref, other_ref,
    out_ref, first_ref, last_ref, field_ref,
):
    vecs, levs, rows, lon = q_ref.shape
    row = lax.broadcasted_iota(jnp.int32, (rows, lon), 0)
    mask = mask_ref[...].astype(jnp.float32)
    own_column = column_ref[0]

    def level_step(level, carry):
        for own in range(COLUMNS):

            @pl.when(own_column == own)
            def _():
                for half in range(2):
                    for k, tile, lo, hi, column, at in field_parts(rows, half):
                        piece_ref = own_ref if column == own else other_ref
                        field_ref[k, lo:hi, tile * LANES : (tile + 1) * LANES] = piece_ref[
                            level * 2 + half, at : at + hi - lo
                        ].astype(jnp.float32)

        f0, f1, f2 = (field_ref[k, :, :lon] for k in range(FIELDS))
        up = jnp.maximum(level - 1, 0)
        low = jnp.minimum(level + 1, levs - 1)
        for v in range(vecs):
            c = q_ref[v, level]
            n = jnp.where(row == rows - 1, north_ref[v, pl.ds(level, 1)], pltpu.roll(c, rows - 1, 0))
            s = jnp.where(row == 0, south_ref[v, pl.ds(level, 1)], pltpu.roll(c, 1, 0))
            new = advance(c, n, s, q_ref[v, up], q_ref[v, low], f0, f1, f2, mask)
            out_ref[v, level] = new
            first_ref[v, pl.ds(level, 1)] = new[:1]
            last_ref[v, pl.ds(level, 1)] = new[rows - 1 :]
        return carry

    lax.fori_loop(0, levs, level_step, 0)


def one_hour(column, q, south, north, mask, own, other):
    vecs, levs, rows, lon = q.shape
    vmem = pl.BlockSpec(memory_space=pltpu.VMEM)
    edge = jax.ShapeDtypeStruct((vecs, levs, lon), jnp.float32)
    return pl.pallas_call(
        hour_kernel,
        out_shape=(jax.ShapeDtypeStruct(q.shape, jnp.float32), edge, edge),
        in_specs=[pl.BlockSpec(memory_space=pltpu.SMEM)] + [vmem] * 6,
        out_specs=(vmem, vmem, vmem),
        scratch_shapes=[pltpu.VMEM((FIELDS, rows, 6 * LANES), jnp.float32)],
        compiler_params=pltpu.CompilerParams(vmem_limit_bytes=VMEM_LIMIT),
        cost_estimate=pl.CostEstimate(flops=25 * q.size, bytes_accessed=8 * q.size, transcendentals=0),
        name="one_hour",
    )(column, q, south, north, mask, own, other)


def shards(perturb, trajectory, hour_slot, sea_mask):
    lat = lax.axis_size("lat")
    column = lax.axis_index("vec") // RING
    northward = [(i, i + 1) for i in range(lat - 1)]
    southward = [(i + 1, i) for i in range(lat - 1)]
    rings = [[c * RING + z for z in range(RING)] for c in range(COLUMNS)]
    swap = [(i, (i + RING) % (COLUMNS * RING)) for i in range(COLUMNS * RING)]

    def halos(first, last):
        return lax.ppermute(last, "lat", northward), lax.ppermute(first, "lat", southward)

    pieces = lax.all_to_all(pack(trajectory), "vec", 0, 0, tiled=True)
    picked = jnp.stack([lax.dynamic_index_in_dim(pieces, hour_slot[h], 0, keepdims=False) for h in range(2)])
    gathered = lax.all_gather(picked, "vec", axis=0, axis_index_groups=rings)
    own = [gathered[:, h] for h in range(2)]
    other = [lax.ppermute(half, "vec", swap) for half in own]

    q = perturb
    first, last = q[:, :, 0], q[:, :, -1]
    which = column.astype(jnp.int32)[None]
    for h in range(2):
        south, north = halos(first, last)
        q, first, last = one_hour(which, q, south, north, sea_mask, own[h], other[h])
    return q


def solution(mesh):
    return jax.shard_map(
        shards,
        mesh=mesh,
        in_specs=(
            P("vec", None, "lat", None),
            P("vec", None, None, "lat", None),
            P(),
            P("lat", None),
        ),
        out_specs=P("vec", None, "lat", None),
        check_vma=False,
    )
```

```python
import jax
import jax.numpy as jnp
from jax import lax
from jax.experimental import pallas as pl
from jax.experimental.pallas import tpu as pltpu
from jax.sharding import PartitionSpec as P

COLUMNS = 2
RING = 16
LANES = 128
FIELDS = 3
CUT = 40
PIECE = 112
VMEM_LIMIT = 48 * 1024 * 1024


def tile_parts(rows, half):
    total = FIELDS * rows
    base = 3 * half
    return (
        (base, 0, total, 0, 0),
        (base + 1, 0, CUT, 0, total),
        (base + 1, CUT, total, 1, 0),
        (base + 2, 0, total, 1, total - CUT),
    )


def field_parts(rows, half):
    parts = []
    for tile, start, stop, column, at in tile_parts(rows, half):
        for k in range(FIELDS):
            lo, hi = max(start, k * rows), min(stop, (k + 1) * rows)
            if lo < hi:
                parts.append((k, tile, lo - k * rows, hi - k * rows, column, at + lo - start))
    return parts


def pack_kernel(field_ref, piece_ref):
    _, levs, rows, lon = field_ref.shape[1:]
    for level in range(levs):
        for half in range(2):
            for k, tile, lo, hi, column, at in field_parts(rows, half):
                p = column * RING + level * 2 + half
                left, right = tile * LANES, min((tile + 1) * LANES, lon)
                piece_ref[p, at : at + hi - lo, : right - left] = field_ref[0, k, level, lo:hi, left:right]


def pack(trajectory):
    return pl.pallas_call(
        pack_kernel,
        out_shape=jax.ShapeDtypeStruct((COLUMNS * RING, PIECE, LANES), trajectory.dtype),
        in_specs=[pl.BlockSpec(memory_space=pltpu.VMEM)],
        out_specs=pl.BlockSpec(memory_space=pltpu.VMEM),
        compiler_params=pltpu.CompilerParams(vmem_limit_bytes=VMEM_LIMIT),
        name="pack",
    )(trajectory)


def lanes_next(x):
    return jnp.concatenate([x[..., 1:], x[..., :1]], axis=-1)


def lanes_prev(x):
    return jnp.concatenate([x[..., -1:], x[..., :-1]], axis=-1)


def weights(f0, f1, f2, mask):
    diffuse = mask * (0.06 + 0.015 * f0)
    zonal, merid = mask * (0.15 * f1), mask * (0.15 * f2)
    return (
        0.8 * mask - 4.0 * diffuse,
        diffuse - zonal,
        diffuse + zonal,
        diffuse - merid,
        diffuse + merid,
        0.1 * mask,
    )


def advance(c, n, s, u, b, weight):
    wc, we, ww, wn, ws, wl = weight
    return (wc * c + we * lanes_next(c) + ww * lanes_prev(c)) + (wn * n + ws * s + wl * (u + b))


def rows_kernel(
    column_ref, q_ref, south_ref, north_ref, mask_ref, own_ref, other_ref, first_ref, last_ref, field_ref
):
    vecs, levs, rows, lon = q_ref.shape
    lev = lax.broadcasted_iota(jnp.int32, (levs, lon), 0)
    own_column = column_ref[0]

    def row_of(v, r):
        return jnp.concatenate([q_ref[v, z, r : r + 1] for z in range(levs)], axis=0)

    for out_ref, r, step in ((first_ref, 0, 1), (last_ref, rows - 1, -1)):
        for own in range(COLUMNS):

            @pl.when(own_column == own)
            def _():
                for half in range(2):
                    for k, tile, lo, hi, column, at in field_parts(rows, half):
                        if lo <= r < hi:
                            piece_ref = own_ref if column == own else other_ref
                            base = at + (r - lo) // 8 * 8
                            for z in range(levs):
                                eight = piece_ref[z * 2 + half, base : base + 8].astype(jnp.float32)
                                i = (r - lo) % 8
                                field_ref[k, z : z + 1, tile * LANES : (tile + 1) * LANES] = eight[i : i + 1]

        weight = weights(*(field_ref[k, :, :lon] for k in range(FIELDS)), mask_ref[r : r + 1].astype(jnp.float32))
        for v in range(vecs):
            c, inner = row_of(v, r), row_of(v, r + step)
            n, s = (inner, south_ref[v]) if r == 0 else (north_ref[v], inner)
            u = jnp.where(lev == 0, c, pltpu.roll(c, 1, 0))
            b = jnp.where(lev == levs - 1, c, pltpu.roll(c, levs - 1, 0))
            out_ref[v] = advance(c, n, s, u, b, weight)


def hour_kernel(
    column_ref, q_ref, south_ref, north_ref, mask_ref, own_ref, other_ref, out_ref, field_ref
):
    vecs, levs, rows, lon = q_ref.shape
    row = lax.broadcasted_iota(jnp.int32, (rows, lon), 0)
    mask = mask_ref[...].astype(jnp.float32)
    own_column = column_ref[0]

    def level_step(level, carry):
        for own in range(COLUMNS):

            @pl.when(own_column == own)
            def _():
                for half in range(2):
                    for k, tile, lo, hi, column, at in field_parts(rows, half):
                        piece_ref = own_ref if column == own else other_ref
                        field_ref[k, lo:hi, tile * LANES : (tile + 1) * LANES] = piece_ref[
                            level * 2 + half, at : at + hi - lo
                        ].astype(jnp.float32)

        weight = weights(*(field_ref[k, :, :lon] for k in range(FIELDS)), mask)
        up = jnp.maximum(level - 1, 0)
        low = jnp.minimum(level + 1, levs - 1)
        for v in range(vecs):
            c = q_ref[v, level]
            n = jnp.where(row == rows - 1, north_ref[v, pl.ds(level, 1)], pltpu.roll(c, rows - 1, 0))
            s = jnp.where(row == 0, south_ref[v, pl.ds(level, 1)], pltpu.roll(c, 1, 0))
            out_ref[v, level] = advance(c, n, s, q_ref[v, up], q_ref[v, low], weight)
        return carry

    lax.fori_loop(0, levs, level_step, 0)


def on_band(kernel, name, outs, field_rows, flops, args):
    vmem = pl.BlockSpec(memory_space=pltpu.VMEM)
    lon = args[1].shape[-1]
    bytes_accessed = sum(a.size * a.dtype.itemsize for a in (*args, *outs))
    return pl.pallas_call(
        kernel,
        out_shape=outs,
        in_specs=[pl.BlockSpec(memory_space=pltpu.SMEM)] + [vmem] * (len(args) - 1),
        out_specs=tuple(vmem for _ in outs),
        scratch_shapes=[pltpu.VMEM((FIELDS, field_rows, -(-lon // LANES) * LANES), jnp.float32)],
        compiler_params=pltpu.CompilerParams(vmem_limit_bytes=VMEM_LIMIT),
        cost_estimate=pl.CostEstimate(flops=flops, bytes_accessed=bytes_accessed, transcendentals=0),
        name=name,
    )(*args)


def edge_rows(*args):
    vecs, levs, _, lon = args[1].shape
    edge = jax.ShapeDtypeStruct((vecs, levs, lon), jnp.float32)
    return on_band(rows_kernel, "edge_rows", (edge, edge), levs, 30 * edge.size, args)


def one_hour(*args):
    q = args[1]
    return on_band(
        hour_kernel, "one_hour", (jax.ShapeDtypeStruct(q.shape, q.dtype),), q.shape[2], 20 * q.size, args
    )[0]


def shards(perturb, trajectory, hour_slot, sea_mask):
    lat = lax.axis_size("lat")
    column = lax.axis_index("vec") // RING
    northward = [(i, i + 1) for i in range(lat - 1)]
    southward = [(i + 1, i) for i in range(lat - 1)]
    rings = [[c * RING + z for z in range(RING)] for c in range(COLUMNS)]
    swap = [(i, (i + RING) % (COLUMNS * RING)) for i in range(COLUMNS * RING)]

    def halos(first, last):
        return lax.ppermute(last, "lat", northward), lax.ppermute(first, "lat", southward)

    which = column.astype(jnp.int32)[None]
    halo = halos(perturb[:, :, 0], perturb[:, :, -1])

    pieces = lax.all_to_all(pack(trajectory), "vec", 0, 0, tiled=True)
    picked = jnp.stack([lax.dynamic_index_in_dim(pieces, hour_slot[h], 0, keepdims=False) for h in range(2)])
    picked = picked + (sum(h[0, 0, 0] for h in halo) * 0).astype(picked.dtype)
    gathered = lax.all_gather(picked, "vec", axis=0, axis_index_groups=rings)
    own = [gathered[:, h] for h in range(2)]
    other = [lax.ppermute(half, "vec", swap) for half in own]

    args = (which, perturb, *halo, sea_mask, own[0], other[0])
    halo = halos(*edge_rows(*args))
    return one_hour(which, one_hour(*args), *halo, sea_mask, own[1], other[1])


def solution(mesh):
    return jax.shard_map(
        shards,
        mesh=mesh,
        in_specs=(
            P("vec", None, "lat", None),
            P("vec", None, None, "lat", None),
            P(),
            P("lat", None),
        ),
        out_specs=P("vec", None, "lat", None),
        check_vma=False,
    )
```

```python
import jax
import jax.numpy as jnp
from jax import lax
from jax.experimental import pallas as pl
from jax.experimental.pallas import tpu as pltpu
from jax.sharding import PartitionSpec as P

COLUMNS = 2
RING = 16
LANES = 128
FIELDS = 3
CUT = 40
PIECE = 112
VMEM_LIMIT = 48 * 1024 * 1024


def tile_parts(rows, half):
    total = FIELDS * rows
    base = 3 * half
    return (
        (base, 0, total, 0, 0),
        (base + 1, 0, CUT, 0, total),
        (base + 1, CUT, total, 1, 0),
        (base + 2, 0, total, 1, total - CUT),
    )


def field_parts(rows, half):
    parts = []
    for tile, start, stop, column, at in tile_parts(rows, half):
        for k in range(FIELDS):
            lo, hi = max(start, k * rows), min(stop, (k + 1) * rows)
            if lo < hi:
                parts.append((k, tile, lo - k * rows, hi - k * rows, column, at + lo - start))
    return parts


def pack_kernel(column_ref, field_ref, keep_ref, send_ref):
    _, levs, rows, lon = field_ref.shape[1:]
    for own in range(COLUMNS):

        @pl.when(column_ref[0] == own)
        def _():
            for level in range(levs):
                for half in range(2):
                    for k, tile, lo, hi, column, at in field_parts(rows, half):
                        piece_ref = keep_ref if column == own else send_ref
                        left, right = tile * LANES, min((tile + 1) * LANES, lon)
                        piece_ref[level * 2 + half, at : at + hi - lo, : right - left] = field_ref[
                            0, k, level, lo:hi, left:right
                        ]


def pack(column, trajectory):
    half = jax.ShapeDtypeStruct((RING, PIECE, LANES), trajectory.dtype)
    vmem = pl.BlockSpec(memory_space=pltpu.VMEM)
    return pl.pallas_call(
        pack_kernel,
        out_shape=(half, half),
        in_specs=[pl.BlockSpec(memory_space=pltpu.SMEM), vmem],
        out_specs=(vmem, vmem),
        compiler_params=pltpu.CompilerParams(vmem_limit_bytes=VMEM_LIMIT),
        name="pack",
    )(column, trajectory)


def lanes_next(x):
    return jnp.concatenate([x[..., 1:], x[..., :1]], axis=-1)


def lanes_prev(x):
    return jnp.concatenate([x[..., -1:], x[..., :-1]], axis=-1)


def weights(f0, f1, f2, mask):
    diffuse = mask * (0.06 + 0.015 * f0)
    zonal, merid = mask * (0.15 * f1), mask * (0.15 * f2)
    return (
        0.8 * mask - 4.0 * diffuse,
        diffuse - zonal,
        diffuse + zonal,
        diffuse - merid,
        diffuse + merid,
        0.1 * mask,
    )


def advance(c, n, s, u, b, weight):
    wc, we, ww, wn, ws, wl = weight
    return (wc * c + we * lanes_next(c) + ww * lanes_prev(c)) + (wn * n + ws * s + wl * (u + b))


def rows_kernel(
    column_ref, q_ref, south_ref, north_ref, mask_ref, own_ref, other_ref, first_ref, last_ref, field_ref
):
    vecs, levs, rows, lon = q_ref.shape
    lev = lax.broadcasted_iota(jnp.int32, (levs, lon), 0)
    own_column = column_ref[0]

    def row_of(v, r):
        return jnp.concatenate([q_ref[v, z, r : r + 1] for z in range(levs)], axis=0)

    for out_ref, r, step in ((first_ref, 0, 1), (last_ref, rows - 1, -1)):
        for own in range(COLUMNS):

            @pl.when(own_column == own)
            def _():
                for half in range(2):
                    for k, tile, lo, hi, column, at in field_parts(rows, half):
                        if lo <= r < hi:
                            piece_ref = own_ref if column == own else other_ref
                            base = at + (r - lo) // 8 * 8
                            for z in range(levs):
                                eight = piece_ref[z * 2 + half, base : base + 8].astype(jnp.float32)
                                i = (r - lo) % 8
                                field_ref[k, z : z + 1, tile * LANES : (tile + 1) * LANES] = eight[i : i + 1]

        weight = weights(*(field_ref[k, :, :lon] for k in range(FIELDS)), mask_ref[r : r + 1].astype(jnp.float32))
        for v in range(vecs):
            c, inner = row_of(v, r), row_of(v, r + step)
            n, s = (inner, south_ref[v]) if r == 0 else (north_ref[v], inner)
            u = jnp.where(lev == 0, c, pltpu.roll(c, 1, 0))
            b = jnp.where(lev == levs - 1, c, pltpu.roll(c, levs - 1, 0))
            out_ref[v] = advance(c, n, s, u, b, weight)


def hour_kernel(
    column_ref, q_ref, south_ref, north_ref, mask_ref, own_ref, other_ref, out_ref, field_ref
):
    vecs, levs, rows, lon = q_ref.shape
    row = lax.broadcasted_iota(jnp.int32, (rows, lon), 0)
    mask = mask_ref[...].astype(jnp.float32)
    own_column = column_ref[0]

    def level_step(level, carry):
        for own in range(COLUMNS):

            @pl.when(own_column == own)
            def _():
                for half in range(2):
                    for k, tile, lo, hi, column, at in field_parts(rows, half):
                        piece_ref = own_ref if column == own else other_ref
                        field_ref[k, lo:hi, tile * LANES : (tile + 1) * LANES] = piece_ref[
                            level * 2 + half, at : at + hi - lo
                        ].astype(jnp.float32)

        weight = weights(*(field_ref[k, :, :lon] for k in range(FIELDS)), mask)
        up = jnp.maximum(level - 1, 0)
        low = jnp.minimum(level + 1, levs - 1)
        for v in range(vecs):
            c = q_ref[v, level]
            n = jnp.where(row == rows - 1, north_ref[v, pl.ds(level, 1)], pltpu.roll(c, rows - 1, 0))
            s = jnp.where(row == 0, south_ref[v, pl.ds(level, 1)], pltpu.roll(c, 1, 0))
            out_ref[v, level] = advance(c, n, s, q_ref[v, up], q_ref[v, low], weight)
        return carry

    lax.fori_loop(0, levs, level_step, 0)


def on_band(kernel, name, outs, field_rows, flops, args):
    vmem = pl.BlockSpec(memory_space=pltpu.VMEM)
    lon = args[1].shape[-1]
    bytes_accessed = sum(a.size * a.dtype.itemsize for a in (*args, *outs))
    return pl.pallas_call(
        kernel,
        out_shape=outs,
        in_specs=[pl.BlockSpec(memory_space=pltpu.SMEM)] + [vmem] * (len(args) - 1),
        out_specs=tuple(vmem for _ in outs),
        scratch_shapes=[pltpu.VMEM((FIELDS, field_rows, -(-lon // LANES) * LANES), jnp.float32)],
        compiler_params=pltpu.CompilerParams(vmem_limit_bytes=VMEM_LIMIT),
        cost_estimate=pl.CostEstimate(flops=flops, bytes_accessed=bytes_accessed, transcendentals=0),
        name=name,
    )(*args)


def edge_rows(*args):
    vecs, levs, _, lon = args[1].shape
    edge = jax.ShapeDtypeStruct((vecs, levs, lon), jnp.float32)
    return on_band(rows_kernel, "edge_rows", (edge, edge), levs, 30 * edge.size, args)


def one_hour(*args):
    q = args[1]
    return on_band(
        hour_kernel, "one_hour", (jax.ShapeDtypeStruct(q.shape, q.dtype),), q.shape[2], 20 * q.size, args
    )[0]


def shards(perturb, trajectory, hour_slot, sea_mask):
    lat = lax.axis_size("lat")
    column = lax.axis_index("vec") // RING
    northward = [(i, i + 1) for i in range(lat - 1)]
    southward = [(i + 1, i) for i in range(lat - 1)]
    rings = [[c * RING + z for z in range(RING)] for c in range(COLUMNS)]
    swap = [(i, (i + RING) % (COLUMNS * RING)) for i in range(COLUMNS * RING)]

    def halos(first, last):
        return lax.ppermute(last, "lat", northward), lax.ppermute(first, "lat", southward)

    which = column.astype(jnp.int32)[None]
    halo = halos(perturb[:, :, 0], perturb[:, :, -1])

    end, last_hour = RING - 1, COLUMNS * RING - 1
    spare = end - 1
    keep, send = pack(which, trajectory)
    crossed = lax.ppermute(send, "vec", [p for p in swap if p[0] != end])
    moved = jnp.where(
        column == 0,
        lax.ppermute(keep, "vec", [(end, spare)]),
        lax.ppermute(send, "vec", [(end, RING + spare)]),
    )
    asked = hour_slot[0] + hour_slot[1] - last_hour
    z = lax.axis_index("vec") % RING
    from_column = jnp.where(z == end, 1, asked // RING)
    offered = jnp.where(
        (z == spare) & (asked == end), moved, jnp.where(from_column == column, keep, crossed)
    )
    place = jnp.where(hour_slot == end, spare, hour_slot % RING)

    pieces = lax.all_to_all(offered, "vec", 0, 0, axis_index_groups=rings, tiled=True)
    picked = jnp.stack([lax.dynamic_index_in_dim(pieces, place[h], 0, keepdims=False) for h in range(2)])
    picked = picked + (sum(h[0, 0, 0] for h in halo) * 0).astype(picked.dtype)
    gathered = lax.all_gather(picked, "vec", axis=0, axis_index_groups=rings)
    own = [gathered[:, h] for h in range(2)]
    other = [lax.ppermute(half, "vec", swap) for half in own]

    args = (which, perturb, *halo, sea_mask, own[0], other[0])
    halo = halos(*edge_rows(*args))
    return one_hour(which, one_hour(*args), *halo, sea_mask, own[1], other[1])


def solution(mesh):
    return jax.shard_map(
        shards,
        mesh=mesh,
        in_specs=(
            P("vec", None, "lat", None),
            P("vec", None, None, "lat", None),
            P(),
            P("lat", None),
        ),
        out_specs=P("vec", None, "lat", None),
        check_vma=False,
    )
```

```python
import jax
import jax.numpy as jnp
from jax import lax
from jax.experimental import pallas as pl
from jax.experimental.pallas import tpu as pltpu
from jax.sharding import PartitionSpec as P

COLUMNS = 2
RING = 16
LANES = 128
FIELDS = 3
CUT = 40
PIECE = 112
VMEM_LIMIT = 48 * 1024 * 1024


def tile_parts(rows, half):
    total = FIELDS * rows
    base = 3 * half
    return (
        (base, 0, total, 0, 0),
        (base + 1, 0, CUT, 0, total),
        (base + 1, CUT, total, 1, 0),
        (base + 2, 0, total, 1, total - CUT),
    )


def field_parts(rows, half):
    parts = []
    for tile, start, stop, column, at in tile_parts(rows, half):
        for k in range(FIELDS):
            lo, hi = max(start, k * rows), min(stop, (k + 1) * rows)
            if lo < hi:
                parts.append((k, tile, lo - k * rows, hi - k * rows, column, at + lo - start))
    return parts


def pack_kernel(column_ref, field_ref, keep_ref, send_ref):
    _, levs, rows, lon = field_ref.shape[1:]
    for own in range(COLUMNS):

        @pl.when(column_ref[0] == own)
        def _():
            for level in range(levs):
                for half in range(2):
                    for k, tile, lo, hi, column, at in field_parts(rows, half):
                        piece_ref = keep_ref if column == own else send_ref
                        left, right = tile * LANES, min((tile + 1) * LANES, lon)
                        piece_ref[level * 2 + half, at : at + hi - lo, : right - left] = field_ref[
                            0, k, level, lo:hi, left:right
                        ]


def pack(column, trajectory):
    half = jax.ShapeDtypeStruct((RING, PIECE, LANES), trajectory.dtype)
    vmem = pl.BlockSpec(memory_space=pltpu.VMEM)
    return pl.pallas_call(
        pack_kernel,
        out_shape=(half, half),
        in_specs=[pl.BlockSpec(memory_space=pltpu.SMEM), vmem],
        out_specs=(vmem, vmem),
        compiler_params=pltpu.CompilerParams(vmem_limit_bytes=VMEM_LIMIT),
        name="pack",
    )(column, trajectory)


def lanes_next(x):
    return jnp.concatenate([x[..., 1:], x[..., :1]], axis=-1)


def lanes_prev(x):
    return jnp.concatenate([x[..., -1:], x[..., :-1]], axis=-1)


def weights(f0, f1, f2, mask):
    diffuse = mask * (0.06 + 0.015 * f0)
    zonal, merid = mask * (0.15 * f1), mask * (0.15 * f2)
    return (
        0.8 * mask - 4.0 * diffuse,
        diffuse - zonal,
        diffuse + zonal,
        diffuse - merid,
        diffuse + merid,
        0.1 * mask,
    )


def advance(c, n, s, u, b, weight):
    wc, we, ww, wn, ws, wl = weight
    return (wc * c + we * lanes_next(c) + ww * lanes_prev(c)) + (wn * n + ws * s + wl * (u + b))


def rows_kernel(
    column_ref, q_ref, south_ref, north_ref, mask_ref, own_ref, other_ref, first_ref, last_ref, field_ref
):
    vecs, levs, rows, lon = q_ref.shape
    lev = lax.broadcasted_iota(jnp.int32, (levs, lon), 0)
    own_column = column_ref[0]

    def row_of(v, r):
        return jnp.concatenate([q_ref[v, z, r : r + 1] for z in range(levs)], axis=0)

    for out_ref, r, step in ((first_ref, 0, 1), (last_ref, rows - 1, -1)):
        for own in range(COLUMNS):

            @pl.when(own_column == own)
            def _():
                for half in range(2):
                    for k, tile, lo, hi, column, at in field_parts(rows, half):
                        if lo <= r < hi:
                            piece_ref = own_ref if column == own else other_ref
                            base = at + (r - lo) // 8 * 8
                            for z in range(levs):
                                eight = piece_ref[z * 2 + half, base : base + 8].astype(jnp.float32)
                                i = (r - lo) % 8
                                field_ref[k, z : z + 1, tile * LANES : (tile + 1) * LANES] = eight[i : i + 1]

        weight = weights(*(field_ref[k, :, :lon] for k in range(FIELDS)), mask_ref[r : r + 1].astype(jnp.float32))
        for v in range(vecs):
            c, inner = row_of(v, r), row_of(v, r + step)
            n, s = (inner, south_ref[v]) if r == 0 else (north_ref[v], inner)
            u = jnp.where(lev == 0, c, pltpu.roll(c, 1, 0))
            b = jnp.where(lev == levs - 1, c, pltpu.roll(c, levs - 1, 0))
            out_ref[v] = advance(c, n, s, u, b, weight)


def hour_kernel(
    column_ref, q_ref, south_ref, north_ref, mask_ref, own_ref, other_ref, out_ref, field_ref
):
    vecs, levs, rows, lon = q_ref.shape
    row = lax.broadcasted_iota(jnp.int32, (rows, lon), 0)
    mask = mask_ref[...].astype(jnp.float32)
    own_column = column_ref[0]

    def level_step(level, carry):
        for own in range(COLUMNS):

            @pl.when(own_column == own)
            def _():
                for half in range(2):
                    for k, tile, lo, hi, column, at in field_parts(rows, half):
                        piece_ref = own_ref if column == own else other_ref
                        field_ref[k, lo:hi, tile * LANES : (tile + 1) * LANES] = piece_ref[
                            level * 2 + half, at : at + hi - lo
                        ].astype(jnp.float32)

        weight = weights(*(field_ref[k, :, :lon] for k in range(FIELDS)), mask)
        up = jnp.maximum(level - 1, 0)
        low = jnp.minimum(level + 1, levs - 1)
        for v in range(vecs):
            c = q_ref[v, level]
            n = jnp.where(row == rows - 1, north_ref[v, pl.ds(level, 1)], pltpu.roll(c, rows - 1, 0))
            s = jnp.where(row == 0, south_ref[v, pl.ds(level, 1)], pltpu.roll(c, 1, 0))
            out_ref[v, level] = advance(c, n, s, q_ref[v, up], q_ref[v, low], weight)
        return carry

    lax.fori_loop(0, levs, level_step, 0)


def on_band(kernel, name, outs, field_rows, flops, args):
    vmem = pl.BlockSpec(memory_space=pltpu.VMEM)
    lon = args[1].shape[-1]
    bytes_accessed = sum(a.size * a.dtype.itemsize for a in (*args, *outs))
    return pl.pallas_call(
        kernel,
        out_shape=outs,
        in_specs=[pl.BlockSpec(memory_space=pltpu.SMEM)] + [vmem] * (len(args) - 1),
        out_specs=tuple(vmem for _ in outs),
        scratch_shapes=[pltpu.VMEM((FIELDS, field_rows, -(-lon // LANES) * LANES), jnp.float32)],
        compiler_params=pltpu.CompilerParams(vmem_limit_bytes=VMEM_LIMIT),
        cost_estimate=pl.CostEstimate(flops=flops, bytes_accessed=bytes_accessed, transcendentals=0),
        name=name,
    )(*args)


def edge_rows(*args):
    vecs, levs, _, lon = args[1].shape
    edge = jax.ShapeDtypeStruct((vecs, levs, lon), jnp.float32)
    return on_band(rows_kernel, "edge_rows", (edge, edge), levs, 30 * edge.size, args)


def one_hour(*args):
    q = args[1]
    return on_band(
        hour_kernel, "one_hour", (jax.ShapeDtypeStruct(q.shape, q.dtype),), q.shape[2], 20 * q.size, args
    )[0]


def shards(perturb, trajectory, hour_slot, sea_mask):
    lat = lax.axis_size("lat")
    column = lax.axis_index("vec") // RING
    northward = [(i, i + 1) for i in range(lat - 1)]
    southward = [(i + 1, i) for i in range(lat - 1)]
    rings = [[c * RING + z for z in range(RING)] for c in range(COLUMNS)]
    swap = [(i, (i + RING) % (COLUMNS * RING)) for i in range(COLUMNS * RING)]

    def halos(first, last):
        return lax.ppermute(last, "lat", northward), lax.ppermute(first, "lat", southward)

    which = column.astype(jnp.int32)[None]
    halo = halos(perturb[:, :, 0], perturb[:, :, -1])

    end, last_hour = RING - 1, COLUMNS * RING - 1
    keep, send = pack(which, trajectory)
    crossed = lax.ppermute(send, "vec", swap)
    moved = lax.ppermute(keep, "vec", [(c * RING + end, c * RING + end - 1) for c in range(COLUMNS)])
    asked = hour_slot[0] + hour_slot[1] - last_hour
    both = asked == end
    z = lax.axis_index("vec") % RING
    own_there = jnp.where(z == end, (column == 1) & ~both, asked // RING == column)
    offered = jnp.where((z == end - 1) & both, moved, jnp.where(own_there, keep, crossed))
    place = jnp.where(both & (hour_slot // RING == column), end - 1, hour_slot % RING)

    pieces = lax.all_to_all(offered, "vec", 0, 0, axis_index_groups=rings, tiled=True)
    picked = jnp.stack([lax.dynamic_index_in_dim(pieces, place[h], 0, keepdims=False) for h in range(2)])
    picked = picked + (sum(h[0, 0, 0] for h in halo) * 0).astype(picked.dtype)
    gathered = lax.all_gather(picked, "vec", axis=0, axis_index_groups=rings)
    own = [gathered[:, h] for h in range(2)]
    other = [lax.ppermute(half, "vec", swap) for half in own]

    args = (which, perturb, *halo, sea_mask, own[0], other[0])
    halo = halos(*edge_rows(*args))
    return one_hour(which, one_hour(*args), *halo, sea_mask, own[1], other[1])


def solution(mesh):
    return jax.shard_map(
        shards,
        mesh=mesh,
        in_specs=(
            P("vec", None, "lat", None),
            P("vec", None, None, "lat", None),
            P(),
            P("lat", None),
        ),
        out_specs=P("vec", None, "lat", None),
        check_vma=False,
    )
```

```python
import jax
import jax.numpy as jnp
from jax import lax
from jax.experimental import pallas as pl
from jax.experimental.pallas import tpu as pltpu
from jax.sharding import PartitionSpec as P

COLUMNS = 2
RING = 16
LANES = 128
FIELDS = 3
CUT = 40
PIECE = 112
VMEM_LIMIT = 48 * 1024 * 1024


def tile_parts(rows, half):
    total = FIELDS * rows
    base = 3 * half
    return (
        (base, 0, total, 0, 0),
        (base + 1, 0, CUT, 0, total),
        (base + 1, CUT, total, 1, 0),
        (base + 2, 0, total, 1, total - CUT),
    )


def field_parts(rows, half):
    parts = []
    for tile, start, stop, column, at in tile_parts(rows, half):
        for k in range(FIELDS):
            lo, hi = max(start, k * rows), min(stop, (k + 1) * rows)
            if lo < hi:
                parts.append((k, tile, lo - k * rows, hi - k * rows, column, at + lo - start))
    return parts


def pack_kernel(place_ref, field_ref, keep_ref, send_ref):
    _, levs, rows, lon = field_ref.shape[1:]
    for own in range(COLUMNS):

        @pl.when(place_ref[0] == own)
        def _():
            for level in range(levs):
                for half in range(2):
                    for k, tile, lo, hi, column, at in field_parts(rows, half):
                        piece_ref = keep_ref if column == own else send_ref
                        left, right = tile * LANES, min((tile + 1) * LANES, lon)
                        piece_ref[level * 2 + half, at : at + hi - lo, : right - left] = field_ref[
                            0, k, level, lo:hi, left:right
                        ]


def pack(place, trajectory):
    half = jax.ShapeDtypeStruct((RING, PIECE, LANES), trajectory.dtype)
    vmem = pl.BlockSpec(memory_space=pltpu.VMEM)
    return pl.pallas_call(
        pack_kernel,
        out_shape=(half, half),
        in_specs=[pl.BlockSpec(memory_space=pltpu.SMEM), vmem],
        out_specs=(vmem, vmem),
        compiler_params=pltpu.CompilerParams(vmem_limit_bytes=VMEM_LIMIT),
        name="pack",
    )(place, trajectory)


def lanes_next(x):
    return jnp.concatenate([x[..., 1:], x[..., :1]], axis=-1)


def lanes_prev(x):
    return jnp.concatenate([x[..., -1:], x[..., :-1]], axis=-1)


def weights(f0, f1, f2, mask):
    diffuse = mask * (0.06 + 0.015 * f0)
    zonal, merid = mask * (0.15 * f1), mask * (0.15 * f2)
    return (
        0.8 * mask - 4.0 * diffuse,
        diffuse - zonal,
        diffuse + zonal,
        diffuse - merid,
        diffuse + merid,
        0.1 * mask,
    )


def advance(c, n, s, u, b, weight):
    wc, we, ww, wn, ws, wl = weight
    return (wc * c + we * lanes_next(c) + ww * lanes_prev(c)) + (wn * n + ws * s + wl * (u + b))


def neighbours(place_ref, near, far):
    odd = place_ref[1] == 1
    return jnp.where(odd, near, far), jnp.where(odd, far, near)


def rows_kernel(
    place_ref, q_ref, near_ref, far_ref, mask_ref, own_ref, other_ref, to_near_ref, to_far_ref, field_ref
):
    vecs, levs, rows, lon = q_ref.shape
    lev = lax.broadcasted_iota(jnp.int32, (levs, lon), 0)
    own_column, odd = place_ref[0], place_ref[1]

    def row_of(v, r):
        return jnp.concatenate([q_ref[v, z, r : r + 1] for z in range(levs)], axis=0)

    for r, step in ((0, 1), (rows - 1, -1)):
        for own in range(COLUMNS):

            @pl.when(own_column == own)
            def _():
                for half in range(2):
                    for k, tile, lo, hi, column, at in field_parts(rows, half):
                        if lo <= r < hi:
                            piece_ref = own_ref if column == own else other_ref
                            base = at + (r - lo) // 8 * 8
                            for z in range(levs):
                                eight = piece_ref[z * 2 + half, base : base + 8].astype(jnp.float32)
                                i = (r - lo) % 8
                                field_ref[k, z : z + 1, tile * LANES : (tile + 1) * LANES] = eight[i : i + 1]

        weight = weights(*(field_ref[k, :, :lon] for k in range(FIELDS)), mask_ref[r : r + 1].astype(jnp.float32))
        to_near = odd == (1 if r == 0 else 0)
        for v in range(vecs):
            south, north = neighbours(place_ref, near_ref[v], far_ref[v])
            c, inner = row_of(v, r), row_of(v, r + step)
            n, s = (inner, south) if r == 0 else (north, inner)
            u = jnp.where(lev == 0, c, pltpu.roll(c, 1, 0))
            b = jnp.where(lev == levs - 1, c, pltpu.roll(c, levs - 1, 0))
            new = advance(c, n, s, u, b, weight)

            @pl.when(to_near)
            def _():
                to_near_ref[v] = new

            @pl.when(jnp.logical_not(to_near))
            def _():
                to_far_ref[v] = new


def hour_kernel(
    place_ref, q_ref, near_ref, far_ref, mask_ref, own_ref, other_ref, out_ref, field_ref
):
    vecs, levs, rows, lon = q_ref.shape
    row = lax.broadcasted_iota(jnp.int32, (rows, lon), 0)
    mask = mask_ref[...].astype(jnp.float32)
    own_column = place_ref[0]

    def level_step(level, carry):
        for own in range(COLUMNS):

            @pl.when(own_column == own)
            def _():
                for half in range(2):
                    for k, tile, lo, hi, column, at in field_parts(rows, half):
                        piece_ref = own_ref if column == own else other_ref
                        field_ref[k, lo:hi, tile * LANES : (tile + 1) * LANES] = piece_ref[
                            level * 2 + half, at : at + hi - lo
                        ].astype(jnp.float32)

        weight = weights(*(field_ref[k, :, :lon] for k in range(FIELDS)), mask)
        up = jnp.maximum(level - 1, 0)
        low = jnp.minimum(level + 1, levs - 1)
        for v in range(vecs):
            c = q_ref[v, level]
            south, north = neighbours(place_ref, near_ref[v, pl.ds(level, 1)], far_ref[v, pl.ds(level, 1)])
            n = jnp.where(row == rows - 1, north, pltpu.roll(c, rows - 1, 0))
            s = jnp.where(row == 0, south, pltpu.roll(c, 1, 0))
            out_ref[v, level] = advance(c, n, s, q_ref[v, up], q_ref[v, low], weight)
        return carry

    lax.fori_loop(0, levs, level_step, 0)


def on_band(kernel, name, outs, field_rows, flops, args):
    vmem = pl.BlockSpec(memory_space=pltpu.VMEM)
    lon = args[1].shape[-1]
    bytes_accessed = sum(a.size * a.dtype.itemsize for a in (*args, *outs))
    return pl.pallas_call(
        kernel,
        out_shape=outs,
        in_specs=[pl.BlockSpec(memory_space=pltpu.SMEM)] + [vmem] * (len(args) - 1),
        out_specs=tuple(vmem for _ in outs),
        scratch_shapes=[pltpu.VMEM((FIELDS, field_rows, -(-lon // LANES) * LANES), jnp.float32)],
        compiler_params=pltpu.CompilerParams(vmem_limit_bytes=VMEM_LIMIT),
        cost_estimate=pl.CostEstimate(flops=flops, bytes_accessed=bytes_accessed, transcendentals=0),
        name=name,
    )(*args)


def edge_rows(*args):
    vecs, levs, _, lon = args[1].shape
    edge = jax.ShapeDtypeStruct((vecs, levs, lon), jnp.float32)
    return on_band(rows_kernel, "edge_rows", (edge, edge), levs, 30 * edge.size, args)


def one_hour(*args):
    q = args[1]
    return on_band(
        hour_kernel, "one_hour", (jax.ShapeDtypeStruct(q.shape, q.dtype),), q.shape[2], 20 * q.size, args
    )[0]


def shards(perturb, trajectory, hour_slot, sea_mask):
    lat = lax.axis_size("lat")
    column = lax.axis_index("vec") // RING
    odd = lax.axis_index("lat") % 2
    on_chip = [(i, i ^ 1) for i in range(lat)]
    between = [pair for i in range(1, lat - 1, 2) for pair in ((i, i + 1), (i + 1, i))]
    rings = [[c * RING + z for z in range(RING)] for c in range(COLUMNS)]
    swap = [(i, (i + RING) % (COLUMNS * RING)) for i in range(COLUMNS * RING)]

    def halos(to_near, to_far):
        far = lax.ppermute(to_far, "lat", between)
        return lax.ppermute(to_near, "lat", on_chip), far

    place_here = jnp.stack([column, odd]).astype(jnp.int32)
    first, last = perturb[:, :, 0], perturb[:, :, -1]
    halo = halos(jnp.where(odd == 1, first, last), jnp.where(odd == 1, last, first))

    end, last_hour = RING - 1, COLUMNS * RING - 1
    keep, send = pack(place_here, trajectory)
    crossed = lax.ppermute(send, "vec", swap)
    moved = lax.ppermute(keep, "vec", [(c * RING + end, c * RING + end - 1) for c in range(COLUMNS)])
    asked = hour_slot[0] + hour_slot[1] - last_hour
    both = asked == end
    z = lax.axis_index("vec") % RING
    own_there = jnp.where(z == end, (column == 1) & ~both, asked // RING == column)
    offered = jnp.where((z == end - 1) & both, moved, jnp.where(own_there, keep, crossed))
    place = jnp.where(both & (hour_slot // RING == column), end - 1, hour_slot % RING)

    pieces = lax.all_to_all(offered, "vec", 0, 0, axis_index_groups=rings, tiled=True)
    picked = jnp.stack([lax.dynamic_index_in_dim(pieces, place[h], 0, keepdims=False) for h in range(2)])
    picked = picked + (sum(h[0, 0, 0] for h in halo) * 0).astype(picked.dtype)
    gathered = lax.all_gather(picked, "vec", axis=0, axis_index_groups=rings)
    own = [gathered[:, h] for h in range(2)]
    other = [lax.ppermute(half, "vec", swap) for half in own]

    args = (place_here, perturb, *halo, sea_mask, own[0], other[0])
    halo = halos(*edge_rows(*args))
    return one_hour(place_here, one_hour(*args), *halo, sea_mask, own[1], other[1])


def solution(mesh):
    return jax.shard_map(
        shards,
        mesh=mesh,
        in_specs=(
            P("vec", None, "lat", None),
            P("vec", None, None, "lat", None),
            P(),
            P("lat", None),
        ),
        out_specs=P("vec", None, "lat", None),
        check_vma=False,
    )
```

```python
import jax
import jax.numpy as jnp
from jax import lax
from jax.experimental import pallas as pl
from jax.experimental.pallas import tpu as pltpu
from jax.sharding import PartitionSpec as P

COLUMNS = 2
RING = 16
LANES = 128
FIELDS = 3
CUT = 40
PIECE = 112
VMEM_LIMIT = 48 * 1024 * 1024


def tile_parts(rows, half):
    total = FIELDS * rows
    base = 3 * half
    return (
        (base, 0, total, 0, 0),
        (base + 1, 0, CUT, 0, total),
        (base + 1, CUT, total, 1, 0),
        (base + 2, 0, total, 1, total - CUT),
    )


def field_parts(rows, half):
    parts = []
    for tile, start, stop, column, at in tile_parts(rows, half):
        for k in range(FIELDS):
            lo, hi = max(start, k * rows), min(stop, (k + 1) * rows)
            if lo < hi:
                parts.append((k, tile, lo - k * rows, hi - k * rows, column, at + lo - start))
    return parts


def pack_kernel(place_ref, field_ref, keep_ref, send_ref):
    _, levs, rows, lon = field_ref.shape[1:]
    for own in range(COLUMNS):

        @pl.when(place_ref[0] == own)
        def _():
            for level in range(levs):
                for half in range(2):
                    for k, tile, lo, hi, column, at in field_parts(rows, half):
                        piece_ref = keep_ref if column == own else send_ref
                        left, right = tile * LANES, min((tile + 1) * LANES, lon)
                        piece_ref[level * 2 + half, at : at + hi - lo, : right - left] = field_ref[
                            0, k, level, lo:hi, left:right
                        ]


def pack(place, trajectory):
    half = jax.ShapeDtypeStruct((RING, PIECE, LANES), trajectory.dtype)
    vmem = pl.BlockSpec(memory_space=pltpu.VMEM)
    return pl.pallas_call(
        pack_kernel,
        out_shape=(half, half),
        in_specs=[pl.BlockSpec(memory_space=pltpu.SMEM), vmem],
        out_specs=(vmem, vmem),
        compiler_params=pltpu.CompilerParams(vmem_limit_bytes=VMEM_LIMIT),
        name="pack",
    )(place, trajectory)


def lanes_next(x):
    return jnp.concatenate([x[..., 1:], x[..., :1]], axis=-1)


def lanes_prev(x):
    return jnp.concatenate([x[..., -1:], x[..., :-1]], axis=-1)


def weights(f0, f1, f2, mask):
    diffuse = mask * (0.06 + 0.015 * f0)
    zonal, merid = mask * (0.15 * f1), mask * (0.15 * f2)
    return (
        0.8 * mask - 4.0 * diffuse,
        diffuse - zonal,
        diffuse + zonal,
        diffuse - merid,
        diffuse + merid,
        0.1 * mask,
    )


def advance(c, n, s, u, b, weight):
    wc, we, ww, wn, ws, wl = weight
    return (wc * c + we * lanes_next(c) + ww * lanes_prev(c)) + (wn * n + ws * s + wl * (u + b))


def set_halos(place_ref, near_ref, far_ref, south_ref, north_ref):
    @pl.when(place_ref[1] == 1)
    def _():
        south_ref[...] = near_ref[...]
        north_ref[...] = far_ref[...]

    @pl.when(place_ref[1] == 0)
    def _():
        south_ref[...] = far_ref[...]
        north_ref[...] = near_ref[...]


def rows_kernel(
    place_ref, q_ref, far_ref, near_ref, mask_ref, own_ref, other_ref,
    to_far_ref, to_near_ref, field_ref, south_ref, north_ref,
):
    vecs, levs, rows, lon = q_ref.shape
    lev = lax.broadcasted_iota(jnp.int32, (levs, lon), 0)
    own_column, odd = place_ref[0], place_ref[1]
    set_halos(place_ref, near_ref, far_ref, south_ref, north_ref)

    def row_of(v, r):
        return jnp.concatenate([q_ref[v, z, r : r + 1] for z in range(levs)], axis=0)

    for r, step in ((0, 1), (rows - 1, -1)):
        for own in range(COLUMNS):

            @pl.when(own_column == own)
            def _():
                for half in range(2):
                    for k, tile, lo, hi, column, at in field_parts(rows, half):
                        if lo <= r < hi:
                            piece_ref = own_ref if column == own else other_ref
                            base = at + (r - lo) // 8 * 8
                            for z in range(levs):
                                eight = piece_ref[z * 2 + half, base : base + 8].astype(jnp.float32)
                                i = (r - lo) % 8
                                field_ref[k, z : z + 1, tile * LANES : (tile + 1) * LANES] = eight[i : i + 1]

        weight = weights(*(field_ref[k, :, :lon] for k in range(FIELDS)), mask_ref[r : r + 1].astype(jnp.float32))
        new = []
        for v in range(vecs):
            c, inner = row_of(v, r), row_of(v, r + step)
            n, s = (inner, south_ref[v]) if r == 0 else (north_ref[v], inner)
            u = jnp.where(lev == 0, c, pltpu.roll(c, 1, 0))
            b = jnp.where(lev == levs - 1, c, pltpu.roll(c, levs - 1, 0))
            new.append(advance(c, n, s, u, b, weight))

        @pl.when(odd == (1 if r == 0 else 0))
        def _():
            for v in range(vecs):
                to_near_ref[v] = new[v]

        @pl.when(odd == (0 if r == 0 else 1))
        def _():
            for v in range(vecs):
                to_far_ref[v] = new[v]


def hour_kernel(
    place_ref, q_ref, far_ref, near_ref, mask_ref, own_ref, other_ref,
    out_ref, field_ref, south_ref, north_ref,
):
    vecs, levs, rows, lon = q_ref.shape
    row = lax.broadcasted_iota(jnp.int32, (rows, lon), 0)
    mask = mask_ref[...].astype(jnp.float32)
    own_column = place_ref[0]
    set_halos(place_ref, near_ref, far_ref, south_ref, north_ref)

    def level_step(level, carry):
        for own in range(COLUMNS):

            @pl.when(own_column == own)
            def _():
                for half in range(2):
                    for k, tile, lo, hi, column, at in field_parts(rows, half):
                        piece_ref = own_ref if column == own else other_ref
                        field_ref[k, lo:hi, tile * LANES : (tile + 1) * LANES] = piece_ref[
                            level * 2 + half, at : at + hi - lo
                        ].astype(jnp.float32)

        weight = weights(*(field_ref[k, :, :lon] for k in range(FIELDS)), mask)
        up = jnp.maximum(level - 1, 0)
        low = jnp.minimum(level + 1, levs - 1)
        for v in range(vecs):
            c = q_ref[v, level]
            n = jnp.where(row == rows - 1, north_ref[v, pl.ds(level, 1)], pltpu.roll(c, rows - 1, 0))
            s = jnp.where(row == 0, south_ref[v, pl.ds(level, 1)], pltpu.roll(c, 1, 0))
            out_ref[v, level] = advance(c, n, s, q_ref[v, up], q_ref[v, low], weight)
        return carry

    lax.fori_loop(0, levs, level_step, 0)


def on_band(kernel, name, outs, field_rows, flops, args):
    vmem = pl.BlockSpec(memory_space=pltpu.VMEM)
    lon = args[1].shape[-1]
    bytes_accessed = sum(a.size * a.dtype.itemsize for a in (*args, *outs))
    return pl.pallas_call(
        kernel,
        out_shape=outs,
        in_specs=[pl.BlockSpec(memory_space=pltpu.SMEM)] + [vmem] * (len(args) - 1),
        out_specs=tuple(vmem for _ in outs),
        scratch_shapes=[
            pltpu.VMEM((FIELDS, field_rows, -(-lon // LANES) * LANES), jnp.float32),
            pltpu.VMEM(args[2].shape, jnp.float32),
            pltpu.VMEM(args[2].shape, jnp.float32),
        ],
        compiler_params=pltpu.CompilerParams(vmem_limit_bytes=VMEM_LIMIT),
        cost_estimate=pl.CostEstimate(flops=flops, bytes_accessed=bytes_accessed, transcendentals=0),
        name=name,
    )(*args)


def edge_rows(*args):
    vecs, levs, _, lon = args[1].shape
    edge = jax.ShapeDtypeStruct((vecs, levs, lon), jnp.float32)
    return on_band(rows_kernel, "edge_rows", (edge, edge), levs, 30 * edge.size, args)


def one_hour(*args):
    q = args[1]
    return on_band(
        hour_kernel, "one_hour", (jax.ShapeDtypeStruct(q.shape, q.dtype),), q.shape[2], 20 * q.size, args
    )[0]


def shards(perturb, trajectory, hour_slot, sea_mask):
    lat = lax.axis_size("lat")
    column = lax.axis_index("vec") // RING
    odd = lax.axis_index("lat") % 2
    on_chip = [(i, i ^ 1) for i in range(lat)]
    between = [pair for i in range(1, lat - 1, 2) for pair in ((i, i + 1), (i + 1, i))]
    rings = [[c * RING + z for z in range(RING)] for c in range(COLUMNS)]
    swap = [(i, (i + RING) % (COLUMNS * RING)) for i in range(COLUMNS * RING)]

    def halos(to_far, to_near):
        far = lax.ppermute(to_far, "lat", between)
        return far, lax.ppermute(to_near, "lat", on_chip)

    place_here = jnp.stack([column, odd]).astype(jnp.int32)
    first, last = perturb[:, :, 0], perturb[:, :, -1]
    halo = halos(jnp.where(odd == 1, last, first), jnp.where(odd == 1, first, last))

    end, last_hour = RING - 1, COLUMNS * RING - 1
    keep, send = pack(place_here, trajectory)
    crossed = lax.ppermute(send, "vec", swap)
    moved = lax.ppermute(keep, "vec", [(c * RING + end, c * RING + end - 1) for c in range(COLUMNS)])
    asked = hour_slot[0] + hour_slot[1] - last_hour
    both = asked == end
    z = lax.axis_index("vec") % RING
    own_there = jnp.where(z == end, (column == 1) & ~both, asked // RING == column)
    offered = jnp.where((z == end - 1) & both, moved, jnp.where(own_there, keep, crossed))
    place = jnp.where(both & (hour_slot // RING == column), end - 1, hour_slot % RING)

    pieces = lax.all_to_all(offered, "vec", 0, 0, axis_index_groups=rings, tiled=True)
    picked = jnp.stack([lax.dynamic_index_in_dim(pieces, place[h], 0, keepdims=False) for h in range(2)])
    picked = picked + (sum(h[0, 0, 0] for h in halo) * 0).astype(picked.dtype)
    gathered = lax.all_gather(picked, "vec", axis=0, axis_index_groups=rings)
    own = [gathered[:, h] for h in range(2)]
    other = [lax.ppermute(own[0], "vec", swap)]
    other.append(lax.ppermute(own[1] + other[0][0, 0, 0] * 0, "vec", swap))

    args = (place_here, perturb, *halo, sea_mask, own[0], other[0])
    halo = halos(*edge_rows(*args))
    return one_hour(place_here, one_hour(*args), *halo, sea_mask, own[1], other[1])


def solution(mesh):
    return jax.shard_map(
        shards,
        mesh=mesh,
        in_specs=(
            P("vec", None, "lat", None),
            P("vec", None, None, "lat", None),
            P(),
            P("lat", None),
        ),
        out_specs=P("vec", None, "lat", None),
        check_vma=False,
    )
```

```python
import jax
import jax.numpy as jnp
from jax import lax
from jax.experimental import pallas as pl
from jax.experimental.pallas import tpu as pltpu
from jax.sharding import PartitionSpec as P

COLUMNS = 2
RING = 16
LANES = 128
FIELDS = 3
CUT = 40
PIECE = 112
VMEM_LIMIT = 48 * 1024 * 1024


def tile_parts(rows, half):
    total = FIELDS * rows
    base = 3 * half
    return (
        (base, 0, total, 0, 0),
        (base + 1, 0, CUT, 0, total),
        (base + 1, CUT, total, 1, 0),
        (base + 2, 0, total, 1, total - CUT),
    )


def field_parts(rows, half):
    parts = []
    for tile, start, stop, column, at in tile_parts(rows, half):
        for k in range(FIELDS):
            lo, hi = max(start, k * rows), min(stop, (k + 1) * rows)
            if lo < hi:
                parts.append((k, tile, lo - k * rows, hi - k * rows, column, at + lo - start))
    return parts


def pack_kernel(place_ref, field_ref, keep_ref, send_ref):
    _, levs, rows, lon = field_ref.shape[1:]
    for own in range(COLUMNS):

        @pl.when(place_ref[0] == own)
        def _():
            for level in range(levs):
                for half in range(2):
                    for k, tile, lo, hi, column, at in field_parts(rows, half):
                        piece_ref = keep_ref if column == own else send_ref
                        left, right = tile * LANES, min((tile + 1) * LANES, lon)
                        piece_ref[level * 2 + half, at : at + hi - lo, : right - left] = field_ref[
                            0, k, level, lo:hi, left:right
                        ]


def pack(place, trajectory):
    half = jax.ShapeDtypeStruct((RING, PIECE, LANES), trajectory.dtype)
    vmem = pl.BlockSpec(memory_space=pltpu.VMEM)
    return pl.pallas_call(
        pack_kernel,
        out_shape=(half, half),
        in_specs=[pl.BlockSpec(memory_space=pltpu.SMEM), vmem],
        out_specs=(vmem, vmem),
        compiler_params=pltpu.CompilerParams(vmem_limit_bytes=VMEM_LIMIT),
        name="pack",
    )(place, trajectory)


def lanes_next(x):
    return jnp.concatenate([x[..., 1:], x[..., :1]], axis=-1)


def lanes_prev(x):
    return jnp.concatenate([x[..., -1:], x[..., :-1]], axis=-1)


def weights(f0, f1, f2, mask):
    diffuse = mask * (0.06 + 0.015 * f0)
    zonal, merid = mask * (0.15 * f1), mask * (0.15 * f2)
    return (
        0.8 * mask - 4.0 * diffuse,
        diffuse - zonal,
        diffuse + zonal,
        diffuse - merid,
        diffuse + merid,
        0.1 * mask,
    )


def advance(c, n, s, u, b, weight):
    wc, we, ww, wn, ws, wl = weight
    return (wc * c + we * lanes_next(c) + ww * lanes_prev(c)) + (wn * n + ws * s + wl * (u + b))


def set_halos(place_ref, near_ref, far_ref, south_ref, north_ref):
    @pl.when(place_ref[1] == 1)
    def _():
        south_ref[...] = near_ref[...]
        north_ref[...] = far_ref[...]

    @pl.when(place_ref[1] == 0)
    def _():
        south_ref[...] = far_ref[...]
        north_ref[...] = near_ref[...]


def rows_kernel(
    place_ref, q_ref, far_ref, near_ref, mask_ref, own_ref, other_ref,
    to_far_ref, to_near_ref, field_ref, south_ref, north_ref,
):
    vecs, levs, rows, lon = q_ref.shape
    lev = lax.broadcasted_iota(jnp.int32, (levs, lon), 0)
    own_column, odd = place_ref[0], place_ref[1]
    set_halos(place_ref, near_ref, far_ref, south_ref, north_ref)

    def row_of(v, r):
        return jnp.concatenate([q_ref[v, z, r : r + 1] for z in range(levs)], axis=0)

    for r, step in ((0, 1), (rows - 1, -1)):
        for own in range(COLUMNS):

            @pl.when(own_column == own)
            def _():
                for half in range(2):
                    for k, tile, lo, hi, column, at in field_parts(rows, half):
                        if lo <= r < hi:
                            piece_ref = own_ref if column == own else other_ref
                            base = at + (r - lo) // 8 * 8
                            for z in range(levs):
                                eight = piece_ref[z * 2 + half, base : base + 8].astype(jnp.float32)
                                i = (r - lo) % 8
                                field_ref[k, z : z + 1, tile * LANES : (tile + 1) * LANES] = eight[i : i + 1]

        weight = weights(*(field_ref[k, :, :lon] for k in range(FIELDS)), mask_ref[r : r + 1].astype(jnp.float32))
        new = []
        for v in range(vecs):
            c, inner = row_of(v, r), row_of(v, r + step)
            n, s = (inner, south_ref[v]) if r == 0 else (north_ref[v], inner)
            u = jnp.where(lev == 0, c, pltpu.roll(c, 1, 0))
            b = jnp.where(lev == levs - 1, c, pltpu.roll(c, levs - 1, 0))
            new.append(advance(c, n, s, u, b, weight))

        @pl.when(odd == (1 if r == 0 else 0))
        def _():
            for v in range(vecs):
                to_near_ref[v] = new[v]

        @pl.when(odd == (0 if r == 0 else 1))
        def _():
            for v in range(vecs):
                to_far_ref[v] = new[v]


def hour_kernel(
    place_ref, q_ref, far_ref, near_ref, mask_ref, own_ref, other_ref,
    out_ref, field_ref, south_ref, north_ref,
):
    vecs, levs, rows, lon = q_ref.shape
    row = lax.broadcasted_iota(jnp.int32, (rows, lon), 0)
    mask = mask_ref[...].astype(jnp.float32)
    own_column = place_ref[0]
    set_halos(place_ref, near_ref, far_ref, south_ref, north_ref)

    def level_step(level, carry):
        for own in range(COLUMNS):

            @pl.when(own_column == own)
            def _():
                for half in range(2):
                    for k, tile, lo, hi, column, at in field_parts(rows, half):
                        piece_ref = own_ref if column == own else other_ref
                        field_ref[k, lo:hi, tile * LANES : (tile + 1) * LANES] = piece_ref[
                            level * 2 + half, at : at + hi - lo
                        ].astype(jnp.float32)

        weight = weights(*(field_ref[k, :, :lon] for k in range(FIELDS)), mask)
        up = jnp.maximum(level - 1, 0)
        low = jnp.minimum(level + 1, levs - 1)
        for v in range(vecs):
            c = q_ref[v, level]
            n = jnp.where(row == rows - 1, north_ref[v, pl.ds(level, 1)], pltpu.roll(c, rows - 1, 0))
            s = jnp.where(row == 0, south_ref[v, pl.ds(level, 1)], pltpu.roll(c, 1, 0))
            out_ref[v, level] = advance(c, n, s, q_ref[v, up], q_ref[v, low], weight)
        return carry

    lax.fori_loop(0, levs, level_step, 0)


def on_band(kernel, name, outs, field_rows, flops, args):
    vmem = pl.BlockSpec(memory_space=pltpu.VMEM)
    lon = args[1].shape[-1]
    bytes_accessed = sum(a.size * a.dtype.itemsize for a in (*args, *outs))
    return pl.pallas_call(
        kernel,
        out_shape=outs,
        in_specs=[pl.BlockSpec(memory_space=pltpu.SMEM)] + [vmem] * (len(args) - 1),
        out_specs=tuple(vmem for _ in outs),
        scratch_shapes=[
            pltpu.VMEM((FIELDS, field_rows, -(-lon // LANES) * LANES), jnp.float32),
            pltpu.VMEM(args[2].shape, jnp.float32),
            pltpu.VMEM(args[2].shape, jnp.float32),
        ],
        compiler_params=pltpu.CompilerParams(vmem_limit_bytes=VMEM_LIMIT),
        cost_estimate=pl.CostEstimate(flops=flops, bytes_accessed=bytes_accessed, transcendentals=0),
        name=name,
    )(*args)


def edge_rows(*args):
    vecs, levs, _, lon = args[1].shape
    edge = jax.ShapeDtypeStruct((vecs, levs, lon), jnp.float32)
    return on_band(rows_kernel, "edge_rows", (edge, edge), levs, 30 * edge.size, args)


def one_hour(*args):
    q = args[1]
    return on_band(
        hour_kernel, "one_hour", (jax.ShapeDtypeStruct(q.shape, q.dtype),), q.shape[2], 20 * q.size, args
    )[0]


def shards(perturb, trajectory, hour_slot, sea_mask):
    lat = lax.axis_size("lat")
    column = lax.axis_index("vec") // RING
    odd = lax.axis_index("lat") % 2
    on_chip = [(i, i ^ 1) for i in range(lat)]
    between = [pair for i in range(1, lat - 1, 2) for pair in ((i, i + 1), (i + 1, i))]
    rings = [[c * RING + z for z in range(RING)] for c in range(COLUMNS)]
    swap = [(i, (i + RING) % (COLUMNS * RING)) for i in range(COLUMNS * RING)]

    def halos(to_far, to_near):
        far = lax.ppermute(to_far, "lat", between)
        return far, lax.ppermute(to_near, "lat", on_chip)

    place_here = jnp.stack([column, odd]).astype(jnp.int32)
    first, last = perturb[:, :, 0], perturb[:, :, -1]
    halo = halos(jnp.where(odd == 1, last, first), jnp.where(odd == 1, first, last))

    end, last_hour = RING - 1, COLUMNS * RING - 1
    keep, send = pack(place_here, trajectory)
    crossed = lax.ppermute(send, "vec", swap)
    moved = lax.ppermute(keep, "vec", [(c * RING + end, c * RING + end - 1) for c in range(COLUMNS)])
    asked = hour_slot[0] + hour_slot[1] - last_hour
    both = asked == end
    z = lax.axis_index("vec") % RING
    own_there = jnp.where(z == end, (column == 1) & ~both, asked // RING == column)
    offered = jnp.where((z == end - 1) & both, moved, jnp.where(own_there, keep, crossed))
    place = jnp.where(both & (hour_slot // RING == column), end - 1, hour_slot % RING)

    pieces = lax.all_to_all(offered, "vec", 0, 0, axis_index_groups=rings, tiled=True)
    picked = jnp.stack([lax.dynamic_index_in_dim(pieces, place[h], 0, keepdims=False) for h in range(2)])
    picked = picked + (sum(h[0, 0, 0] for h in halo) * 0).astype(picked.dtype)
    gathered = lax.all_gather(picked, "vec", axis=0, axis_index_groups=rings)
    own = [gathered[:, h] for h in range(2)]
    other = [lax.ppermute(half, "vec", swap) for half in own]

    args = (place_here, perturb, *halo, sea_mask, own[0], other[0])
    halo = halos(*edge_rows(*args))
    return one_hour(place_here, one_hour(*args), *halo, sea_mask, own[1], other[1])


def solution(mesh):
    return jax.shard_map(
        shards,
        mesh=mesh,
        in_specs=(
            P("vec", None, "lat", None),
            P("vec", None, None, "lat", None),
            P(),
            P("lat", None),
        ),
        out_specs=P("vec", None, "lat", None),
        check_vma=False,
    )
```

```python
import jax
import jax.numpy as jnp
from jax import lax
from jax.experimental import pallas as pl
from jax.experimental.pallas import tpu as pltpu
from jax.sharding import PartitionSpec as P

COLUMNS = 2
RING = 16
LANES = 128
FIELDS = 3
CUT = 40
PIECE = 112
VMEM_LIMIT = 48 * 1024 * 1024


def this_column():
    return lax.axis_index("vec") // RING


def odd_band():
    return lax.axis_index("lat") % 2


def tile_parts(rows, half):
    total = FIELDS * rows
    base = 3 * half
    return (
        (base, 0, total, 0, 0),
        (base + 1, 0, CUT, 0, total),
        (base + 1, CUT, total, 1, 0),
        (base + 2, 0, total, 1, total - CUT),
    )


def field_parts(rows, half):
    parts = []
    for tile, start, stop, column, at in tile_parts(rows, half):
        for k in range(FIELDS):
            lo, hi = max(start, k * rows), min(stop, (k + 1) * rows)
            if lo < hi:
                parts.append((k, tile, lo - k * rows, hi - k * rows, column, at + lo - start))
    return parts


def pack_kernel(field_ref, keep_ref, send_ref):
    _, levs, rows, lon = field_ref.shape[1:]
    for own in range(COLUMNS):

        @pl.when(this_column() == own)
        def _():
            for level in range(levs):
                for half in range(2):
                    for k, tile, lo, hi, column, at in field_parts(rows, half):
                        piece_ref = keep_ref if column == own else send_ref
                        left, right = tile * LANES, min((tile + 1) * LANES, lon)
                        piece_ref[level * 2 + half, at : at + hi - lo, : right - left] = field_ref[
                            0, k, level, lo:hi, left:right
                        ]


def pack(trajectory):
    half = jax.ShapeDtypeStruct((RING, PIECE, LANES), trajectory.dtype)
    vmem = pl.BlockSpec(memory_space=pltpu.VMEM)
    return pl.pallas_call(
        pack_kernel,
        out_shape=(half, half),
        in_specs=[vmem],
        out_specs=(vmem, vmem),
        compiler_params=pltpu.CompilerParams(vmem_limit_bytes=VMEM_LIMIT),
        name="pack",
    )(trajectory)


def lanes_next(x):
    return jnp.concatenate([x[..., 1:], x[..., :1]], axis=-1)


def lanes_prev(x):
    return jnp.concatenate([x[..., -1:], x[..., :-1]], axis=-1)


def weights(f0, f1, f2, mask):
    diffuse = mask * (0.06 + 0.015 * f0)
    zonal, merid = mask * (0.15 * f1), mask * (0.15 * f2)
    return (
        0.8 * mask - 4.0 * diffuse,
        diffuse - zonal,
        diffuse + zonal,
        diffuse - merid,
        diffuse + merid,
        0.1 * mask,
    )


def advance(c, n, s, u, b, weight):
    wc, we, ww, wn, ws, wl = weight
    return (wc * c + we * lanes_next(c) + ww * lanes_prev(c)) + (wn * n + ws * s + wl * (u + b))


def set_halos(near_ref, far_ref, south_ref, north_ref):
    @pl.when(odd_band() == 1)
    def _():
        south_ref[...] = near_ref[...]
        north_ref[...] = far_ref[...]

    @pl.when(odd_band() == 0)
    def _():
        south_ref[...] = far_ref[...]
        north_ref[...] = near_ref[...]


def rows_kernel(
    q_ref, far_ref, near_ref, mask_ref, own_ref, other_ref,
    to_far_ref, to_near_ref, field_ref, south_ref, north_ref,
):
    vecs, levs, rows, lon = q_ref.shape
    lev = lax.broadcasted_iota(jnp.int32, (levs, lon), 0)
    own_column, odd = this_column(), odd_band()
    set_halos(near_ref, far_ref, south_ref, north_ref)

    def row_of(v, r):
        return jnp.concatenate([q_ref[v, z, r : r + 1] for z in range(levs)], axis=0)

    for r, step in ((0, 1), (rows - 1, -1)):
        for own in range(COLUMNS):

            @pl.when(own_column == own)
            def _():
                for half in range(2):
                    for k, tile, lo, hi, column, at in field_parts(rows, half):
                        if lo <= r < hi:
                            piece_ref = own_ref if column == own else other_ref
                            base = at + (r - lo) // 8 * 8
                            for z in range(levs):
                                eight = piece_ref[z * 2 + half, base : base + 8].astype(jnp.float32)
                                i = (r - lo) % 8
                                field_ref[k, z : z + 1, tile * LANES : (tile + 1) * LANES] = eight[i : i + 1]

        weight = weights(*(field_ref[k, :, :lon] for k in range(FIELDS)), mask_ref[r : r + 1].astype(jnp.float32))
        new = []
        for v in range(vecs):
            c, inner = row_of(v, r), row_of(v, r + step)
            n, s = (inner, south_ref[v]) if r == 0 else (north_ref[v], inner)
            u = jnp.where(lev == 0, c, pltpu.roll(c, 1, 0))
            b = jnp.where(lev == levs - 1, c, pltpu.roll(c, levs - 1, 0))
            new.append(advance(c, n, s, u, b, weight))

        @pl.when(odd == (1 if r == 0 else 0))
        def _():
            for v in range(vecs):
                to_near_ref[v] = new[v]

        @pl.when(odd == (0 if r == 0 else 1))
        def _():
            for v in range(vecs):
                to_far_ref[v] = new[v]


def hour_kernel(
    q_ref, far_ref, near_ref, mask_ref, own_ref, other_ref,
    out_ref, field_ref, south_ref, north_ref, new_ref=None, sent=None,
):
    vecs, levs, rows, lon = q_ref.shape
    row = lax.broadcasted_iota(jnp.int32, (rows, lon), 0)
    mask = mask_ref[...].astype(jnp.float32)
    own_column = this_column()
    set_halos(near_ref, far_ref, south_ref, north_ref)
    to_ref = out_ref if new_ref is None else new_ref

    def sending(level):
        return pltpu.make_async_copy(new_ref.at[:, level], out_ref.at[:, level], sent.at[level])

    for level in range(levs):
        for own in range(COLUMNS):

            @pl.when(own_column == own)
            def _():
                for half in range(2):
                    for k, tile, lo, hi, column, at in field_parts(rows, half):
                        piece_ref = own_ref if column == own else other_ref
                        field_ref[k, lo:hi, tile * LANES : (tile + 1) * LANES] = piece_ref[
                            level * 2 + half, at : at + hi - lo
                        ].astype(jnp.float32)

        weight = weights(*(field_ref[k, :, :lon] for k in range(FIELDS)), mask)
        up, low = max(level - 1, 0), min(level + 1, levs - 1)
        for v in range(vecs):
            c = q_ref[v, level]
            n = jnp.where(row == rows - 1, north_ref[v, level : level + 1], pltpu.roll(c, rows - 1, 0))
            s = jnp.where(row == 0, south_ref[v, level : level + 1], pltpu.roll(c, 1, 0))
            to_ref[v, level] = advance(c, n, s, q_ref[v, up], q_ref[v, low], weight)
        if new_ref is not None:
            sending(level).start()

    if new_ref is not None:
        for level in range(levs):
            sending(level).wait()


def on_band(kernel, name, outs, out_space, field_rows, flops, args, scratch=()):
    vmem = pl.BlockSpec(memory_space=pltpu.VMEM)
    lon = args[0].shape[-1]
    bytes_accessed = sum(a.size * a.dtype.itemsize for a in (*args, *outs))
    return pl.pallas_call(
        kernel,
        out_shape=outs,
        in_specs=[vmem] * len(args),
        out_specs=tuple(pl.BlockSpec(memory_space=out_space) for _ in outs),
        scratch_shapes=[
            pltpu.VMEM((FIELDS, field_rows, -(-lon // LANES) * LANES), jnp.float32),
            pltpu.VMEM(args[1].shape, jnp.float32),
            pltpu.VMEM(args[1].shape, jnp.float32),
            *scratch,
        ],
        compiler_params=pltpu.CompilerParams(vmem_limit_bytes=VMEM_LIMIT),
        cost_estimate=pl.CostEstimate(flops=flops, bytes_accessed=bytes_accessed, transcendentals=0),
        name=name,
    )(*args)


def edge_rows(*args):
    vecs, levs, _, lon = args[0].shape
    edge = jax.ShapeDtypeStruct((vecs, levs, lon), jnp.float32)
    return on_band(rows_kernel, "edge_rows", (edge, edge), pltpu.VMEM, levs, 30 * edge.size, args)


def one_hour(*args):
    q = args[0]
    out = jax.ShapeDtypeStruct(q.shape, q.dtype)
    return on_band(hour_kernel, "one_hour", (out,), pltpu.VMEM, q.shape[2], 20 * q.size, args)[0]


def last_hour(*args):
    q = args[0]
    out = jax.ShapeDtypeStruct(q.shape, q.dtype)
    scratch = (pltpu.VMEM(q.shape, q.dtype), pltpu.SemaphoreType.DMA((q.shape[1],)))
    return on_band(hour_kernel, "last_hour", (out,), pl.ANY, q.shape[2], 20 * q.size, args, scratch)[0]


def shards(perturb, trajectory, hour_slot, sea_mask):
    lat = lax.axis_size("lat")
    column = this_column()
    odd = odd_band()
    on_chip = [(i, i ^ 1) for i in range(lat)]
    between = [pair for i in range(1, lat - 1, 2) for pair in ((i, i + 1), (i + 1, i))]
    rings = [[c * RING + z for z in range(RING)] for c in range(COLUMNS)]
    swap = [(i, (i + RING) % (COLUMNS * RING)) for i in range(COLUMNS * RING)]

    def halos(to_far, to_near):
        far = lax.ppermute(to_far, "lat", between)
        return far, lax.ppermute(to_near, "lat", on_chip)

    first, last = perturb[:, :, 0], perturb[:, :, -1]
    halo = halos(jnp.where(odd == 1, last, first), jnp.where(odd == 1, first, last))

    end, last_slot = RING - 1, COLUMNS * RING - 1
    keep, send = pack(trajectory)
    crossed = lax.ppermute(send, "vec", swap)
    moved = lax.ppermute(keep, "vec", [(c * RING + end, c * RING + end - 1) for c in range(COLUMNS)])
    asked = hour_slot[0] + hour_slot[1] - last_slot
    both = asked == end
    z = lax.axis_index("vec") % RING
    own_there = jnp.where(z == end, (column == 1) & ~both, asked // RING == column)
    offered = jnp.where((z == end - 1) & both, moved, jnp.where(own_there, keep, crossed))
    place = jnp.where(both & (hour_slot // RING == column), end - 1, hour_slot % RING)

    pieces = lax.all_to_all(offered, "vec", 0, 0, axis_index_groups=rings, tiled=True)
    picked = jnp.stack([lax.dynamic_index_in_dim(pieces, place[h], 0, keepdims=False) for h in range(2)])
    picked = picked + (sum(h[0, 0, 0] for h in halo) * 0).astype(picked.dtype)
    gathered = lax.all_gather(picked, "vec", axis=0, axis_index_groups=rings)
    own = [gathered[:, h] for h in range(2)]
    other = [lax.ppermute(half, "vec", swap) for half in own]

    args = (perturb, *halo, sea_mask, own[0], other[0])
    halo = halos(*edge_rows(*args))
    return last_hour(one_hour(*args), *halo, sea_mask, own[1], other[1])


def solution(mesh):
    return jax.shard_map(
        shards,
        mesh=mesh,
        in_specs=(
            P("vec", None, "lat", None),
            P("vec", None, None, "lat", None),
            P(),
            P("lat", None),
        ),
        out_specs=P("vec", None, "lat", None),
        check_vma=False,
    )
```

```python
import jax
import jax.numpy as jnp
from jax import lax
from jax.experimental import pallas as pl
from jax.experimental.pallas import tpu as pltpu
from jax.sharding import PartitionSpec as P

COLUMNS = 2
RING = 16
LANES = 128
FIELDS = 3
FULL = 5
TALL = 40
PIECE = 104
VMEM_LIMIT = 48 * 1024 * 1024


def this_column():
    return lax.axis_index("vec") // RING


def odd_band():
    return lax.axis_index("lat") % 2


def level_parts(rows):
    total = FIELDS * rows
    parts = [(t * LANES, LANES, 0, total, t * total, 0) for t in range(FULL)]
    lane, at = FULL * LANES, FULL * total
    parts.append((lane, 64, 0, TALL, at, 0))
    parts.append((lane, 64, TALL, total, at, 64))
    lane, at = lane + 64, at + TALL
    for start in range(0, total, 8):
        down, across = divmod(start // 8, 8)
        parts.append((lane, 16, start, start + 8, at + 8 * down, 16 * across))
    return parts


def field_parts(rows, half):
    parts = []
    for lane, lanes, start, stop, at, at_lane in level_parts(rows):
        for k in range(FIELDS):
            for column in range(COLUMNS):
                top = (half * COLUMNS + column) * PIECE
                lo = max(start, k * rows, start + top - at)
                hi = min(stop, (k + 1) * rows, start + top + PIECE - at)
                if lo < hi:
                    parts.append((k, lane, lanes, lo - k * rows, hi - k * rows, column, at + lo - start - top, at_lane))
    return parts


def pack_kernel(field_ref, keep_ref, send_ref):
    _, levs, rows, lon = field_ref.shape[1:]
    for own in range(COLUMNS):

        @pl.when(this_column() == own)
        def _():
            for level in range(levs):
                for half in range(2):
                    for k, lane, lanes, lo, hi, column, at, at_lane in field_parts(rows, half):
                        piece_ref = keep_ref if column == own else send_ref
                        piece_ref[level * 2 + half, at : at + hi - lo, at_lane : at_lane + lanes] = field_ref[
                            0, k, level, lo:hi, lane : lane + lanes
                        ]


def pack(trajectory):
    half = jax.ShapeDtypeStruct((RING, PIECE, LANES), trajectory.dtype)
    vmem = pl.BlockSpec(memory_space=pltpu.VMEM)
    return pl.pallas_call(
        pack_kernel,
        out_shape=(half, half),
        in_specs=[vmem],
        out_specs=(vmem, vmem),
        compiler_params=pltpu.CompilerParams(vmem_limit_bytes=VMEM_LIMIT),
        name="pack",
    )(trajectory)


def lanes_next(x):
    return jnp.concatenate([x[..., 1:], x[..., :1]], axis=-1)


def lanes_prev(x):
    return jnp.concatenate([x[..., -1:], x[..., :-1]], axis=-1)


def weights(f0, f1, f2, mask):
    diffuse = mask * (0.06 + 0.015 * f0)
    zonal, merid = mask * (0.15 * f1), mask * (0.15 * f2)
    return (
        0.8 * mask - 4.0 * diffuse,
        diffuse - zonal,
        diffuse + zonal,
        diffuse - merid,
        diffuse + merid,
        0.1 * mask,
    )


def advance(c, n, s, u, b, weight):
    wc, we, ww, wn, ws, wl = weight
    return (wc * c + we * lanes_next(c) + ww * lanes_prev(c)) + (wn * n + ws * s + wl * (u + b))


def set_halos(near_ref, far_ref, south_ref, north_ref):
    @pl.when(odd_band() == 1)
    def _():
        south_ref[...] = near_ref[...]
        north_ref[...] = far_ref[...]

    @pl.when(odd_band() == 0)
    def _():
        south_ref[...] = far_ref[...]
        north_ref[...] = near_ref[...]


def rows_kernel(
    q_ref, far_ref, near_ref, mask_ref, own_ref, other_ref,
    to_far_ref, to_near_ref, field_ref, south_ref, north_ref,
):
    vecs, levs, rows, lon = q_ref.shape
    lev = lax.broadcasted_iota(jnp.int32, (levs, lon), 0)
    own_column, odd = this_column(), odd_band()
    set_halos(near_ref, far_ref, south_ref, north_ref)

    def row_of(v, r):
        return jnp.concatenate([q_ref[v, z, r : r + 1] for z in range(levs)], axis=0)

    for r, step in ((0, 1), (rows - 1, -1)):
        for own in range(COLUMNS):

            @pl.when(own_column == own)
            def _():
                for half in range(2):
                    for k, lane, lanes, lo, hi, column, at, at_lane in field_parts(rows, half):
                        if lo <= r < hi:
                            piece_ref = own_ref if column == own else other_ref
                            base = at + (r - lo) // 8 * 8
                            for z in range(levs):
                                eight = piece_ref[z * 2 + half, base : base + 8].astype(jnp.float32)
                                i = (r - lo) % 8
                                field_ref[k, z : z + 1, lane : lane + lanes] = eight[
                                    i : i + 1, at_lane : at_lane + lanes
                                ]

        weight = weights(*(field_ref[k, :, :lon] for k in range(FIELDS)), mask_ref[r : r + 1].astype(jnp.float32))
        new = []
        for v in range(vecs):
            c, inner = row_of(v, r), row_of(v, r + step)
            n, s = (inner, south_ref[v]) if r == 0 else (north_ref[v], inner)
            u = jnp.where(lev == 0, c, pltpu.roll(c, 1, 0))
            b = jnp.where(lev == levs - 1, c, pltpu.roll(c, levs - 1, 0))
            new.append(advance(c, n, s, u, b, weight))

        @pl.when(odd == (1 if r == 0 else 0))
        def _():
            for v in range(vecs):
                to_near_ref[v] = new[v]

        @pl.when(odd == (0 if r == 0 else 1))
        def _():
            for v in range(vecs):
                to_far_ref[v] = new[v]


def hour_kernel(
    q_ref, far_ref, near_ref, mask_ref, own_ref, other_ref,
    out_ref, field_ref, south_ref, north_ref, new_ref=None, sent=None,
):
    vecs, levs, rows, lon = q_ref.shape
    row = lax.broadcasted_iota(jnp.int32, (rows, lon), 0)
    mask = mask_ref[...].astype(jnp.float32)
    own_column = this_column()
    set_halos(near_ref, far_ref, south_ref, north_ref)
    to_ref = out_ref if new_ref is None else new_ref

    def sending(level):
        return pltpu.make_async_copy(new_ref.at[:, level], out_ref.at[:, level], sent.at[level])

    for level in range(levs):
        for own in range(COLUMNS):

            @pl.when(own_column == own)
            def _():
                for half in range(2):
                    for k, lane, lanes, lo, hi, column, at, at_lane in field_parts(rows, half):
                        piece_ref = own_ref if column == own else other_ref
                        part = piece_ref[level * 2 + half, at : at + hi - lo].astype(jnp.float32)
                        field_ref[k, lo:hi, lane : lane + lanes] = part[:, at_lane : at_lane + lanes]

        weight = weights(*(field_ref[k, :, :lon] for k in range(FIELDS)), mask)
        up, low = max(level - 1, 0), min(level + 1, levs - 1)
        for v in range(vecs):
            c = q_ref[v, level]
            n = jnp.where(row == rows - 1, north_ref[v, level : level + 1], pltpu.roll(c, rows - 1, 0))
            s = jnp.where(row == 0, south_ref[v, level : level + 1], pltpu.roll(c, 1, 0))
            to_ref[v, level] = advance(c, n, s, q_ref[v, up], q_ref[v, low], weight)
        if new_ref is not None:
            sending(level).start()

    if new_ref is not None:
        for level in range(levs):
            sending(level).wait()


def on_band(kernel, name, outs, out_space, field_rows, flops, args, scratch=()):
    vmem = pl.BlockSpec(memory_space=pltpu.VMEM)
    lon = args[0].shape[-1]
    bytes_accessed = sum(a.size * a.dtype.itemsize for a in (*args, *outs))
    return pl.pallas_call(
        kernel,
        out_shape=outs,
        in_specs=[vmem] * len(args),
        out_specs=tuple(pl.BlockSpec(memory_space=out_space) for _ in outs),
        scratch_shapes=[
            pltpu.VMEM((FIELDS, field_rows, -(-lon // LANES) * LANES), jnp.float32),
            pltpu.VMEM(args[1].shape, jnp.float32),
            pltpu.VMEM(args[1].shape, jnp.float32),
            *scratch,
        ],
        compiler_params=pltpu.CompilerParams(vmem_limit_bytes=VMEM_LIMIT),
        cost_estimate=pl.CostEstimate(flops=flops, bytes_accessed=bytes_accessed, transcendentals=0),
        name=name,
    )(*args)


def edge_rows(*args):
    vecs, levs, _, lon = args[0].shape
    edge = jax.ShapeDtypeStruct((vecs, levs, lon), jnp.float32)
    return on_band(rows_kernel, "edge_rows", (edge, edge), pltpu.VMEM, levs, 30 * edge.size, args)


def one_hour(*args):
    q = args[0]
    out = jax.ShapeDtypeStruct(q.shape, q.dtype)
    return on_band(hour_kernel, "one_hour", (out,), pltpu.VMEM, q.shape[2], 20 * q.size, args)[0]


def last_hour(*args):
    q = args[0]
    out = jax.ShapeDtypeStruct(q.shape, q.dtype)
    scratch = (pltpu.VMEM(q.shape, q.dtype), pltpu.SemaphoreType.DMA((q.shape[1],)))
    return on_band(hour_kernel, "last_hour", (out,), pl.ANY, q.shape[2], 20 * q.size, args, scratch)[0]


def shards(perturb, trajectory, hour_slot, sea_mask):
    lat = lax.axis_size("lat")
    column = this_column()
    odd = odd_band()
    on_chip = [(i, i ^ 1) for i in range(lat)]
    between = [pair for i in range(1, lat - 1, 2) for pair in ((i, i + 1), (i + 1, i))]
    rings = [[c * RING + z for z in range(RING)] for c in range(COLUMNS)]
    swap = [(i, (i + RING) % (COLUMNS * RING)) for i in range(COLUMNS * RING)]

    def halos(to_far, to_near):
        far = lax.ppermute(to_far, "lat", between)
        return far, lax.ppermute(to_near, "lat", on_chip)

    first, last = perturb[:, :, 0], perturb[:, :, -1]
    halo = halos(jnp.where(odd == 1, last, first), jnp.where(odd == 1, first, last))

    end, last_slot = RING - 1, COLUMNS * RING - 1
    keep, send = pack(trajectory)
    crossed = lax.ppermute(send, "vec", swap)
    moved = lax.ppermute(keep, "vec", [(c * RING + end, c * RING + end - 1) for c in range(COLUMNS)])
    asked = hour_slot[0] + hour_slot[1] - last_slot
    both = asked == end
    z = lax.axis_index("vec") % RING
    own_there = jnp.where(z == end, (column == 1) & ~both, asked // RING == column)
    offered = jnp.where((z == end - 1) & both, moved, jnp.where(own_there, keep, crossed))
    place = jnp.where(both & (hour_slot // RING == column), end - 1, hour_slot % RING)

    pieces = lax.all_to_all(offered, "vec", 0, 0, axis_index_groups=rings, tiled=True)
    picked = jnp.stack([lax.dynamic_index_in_dim(pieces, place[h], 0, keepdims=False) for h in range(2)])
    picked = picked + (sum(h[0, 0, 0] for h in halo) * 0).astype(picked.dtype)
    gathered = lax.all_gather(picked, "vec", axis=0, axis_index_groups=rings)
    own = [gathered[:, h] for h in range(2)]
    other = [lax.ppermute(half, "vec", swap) for half in own]

    args = (perturb, *halo, sea_mask, own[0], other[0])
    halo = halos(*edge_rows(*args))
    return last_hour(one_hour(*args), *halo, sea_mask, own[1], other[1])


def solution(mesh):
    return jax.shard_map(
        shards,
        mesh=mesh,
        in_specs=(
            P("vec", None, "lat", None),
            P("vec", None, None, "lat", None),
            P(),
            P("lat", None),
        ),
        out_specs=P("vec", None, "lat", None),
        check_vma=False,
    )
```

```python
import functools

import jax
import jax.numpy as jnp
from jax import lax
from jax.experimental import pallas as pl
from jax.experimental.pallas import tpu as pltpu
from jax.sharding import PartitionSpec as P

COLUMNS = 2
RING = 16
LANES = 128
FIELDS = 3
FULL = 5
TALL = 40
PIECE = 104
VMEM_LIMIT = 48 * 1024 * 1024


def this_column():
    return lax.axis_index("vec") // RING


def odd_band():
    return lax.axis_index("lat") % 2


def level_parts(rows):
    total = FIELDS * rows
    parts = [(t * LANES, LANES, 0, total, t * total, 0) for t in range(FULL)]
    lane, at = FULL * LANES, FULL * total
    parts.append((lane, 64, 0, TALL, at, 0))
    parts.append((lane, 64, TALL, total, at, 64))
    lane, at = lane + 64, at + TALL
    for start in range(0, total, 8):
        down, across = divmod(start // 8, 8)
        parts.append((lane, 16, start, start + 8, at + 8 * down, 16 * across))
    return parts


def field_parts(rows, half):
    parts = []
    for lane, lanes, start, stop, at, at_lane in level_parts(rows):
        for k in range(FIELDS):
            for column in range(COLUMNS):
                top = (half * COLUMNS + column) * PIECE
                lo = max(start, k * rows, start + top - at)
                hi = min(stop, (k + 1) * rows, start + top + PIECE - at)
                if lo < hi:
                    parts.append((k, lane, lanes, lo - k * rows, hi - k * rows, column, at + lo - start - top, at_lane))
    return parts


def pack_kernel(field_ref, keep_ref, send_ref):
    _, levs, rows, lon = field_ref.shape[1:]
    for own in range(COLUMNS):

        @pl.when(this_column() == own)
        def _():
            for level in range(levs):
                for half in range(2):
                    for k, lane, lanes, lo, hi, column, at, at_lane in field_parts(rows, half):
                        piece_ref = keep_ref if column == own else send_ref
                        piece_ref[level * 2 + half, at : at + hi - lo, at_lane : at_lane + lanes] = field_ref[
                            0, k, level, lo:hi, lane : lane + lanes
                        ]


def pack(trajectory):
    half = jax.ShapeDtypeStruct((RING, PIECE, LANES), trajectory.dtype)
    vmem = pl.BlockSpec(memory_space=pltpu.VMEM)
    return pl.pallas_call(
        pack_kernel,
        out_shape=(half, half),
        in_specs=[vmem],
        out_specs=(vmem, vmem),
        compiler_params=pltpu.CompilerParams(vmem_limit_bytes=VMEM_LIMIT),
        name="pack",
    )(trajectory)


def lanes_next(x):
    return jnp.concatenate([x[..., 1:], x[..., :1]], axis=-1)


def lanes_prev(x):
    return jnp.concatenate([x[..., -1:], x[..., :-1]], axis=-1)


def weights(f0, f1, f2, mask):
    diffuse = mask * (0.06 + 0.015 * f0)
    zonal, merid = mask * (0.15 * f1), mask * (0.15 * f2)
    return (
        0.8 * mask - 4.0 * diffuse,
        diffuse - zonal,
        diffuse + zonal,
        diffuse - merid,
        diffuse + merid,
        0.1 * mask,
    )


def advance(c, n, s, u, b, weight):
    wc, we, ww, wn, ws, wl = weight
    return (wc * c + we * lanes_next(c) + ww * lanes_prev(c)) + (wn * n + ws * s + wl * (u + b))


def set_halos(near_ref, far_ref, south_ref, north_ref):
    @pl.when(odd_band() == 1)
    def _():
        south_ref[...] = near_ref[...]
        north_ref[...] = far_ref[...]

    @pl.when(odd_band() == 0)
    def _():
        south_ref[...] = far_ref[...]
        north_ref[...] = near_ref[...]


def pick_kernel(rows, own_ref, rows_ref, half_ref):
    levs = rows_ref.shape[2]
    half_ref[...] = own_ref[...]
    for own in range(COLUMNS):

        @pl.when(this_column() == own)
        def _():
            for i, r in enumerate((0, rows - 1)):
                for half in range(2):
                    for k, lane, lanes, lo, hi, column, at, at_lane in field_parts(rows, half):
                        if column == own and lo <= r < hi:
                            base, down = at + (r - lo) // 8 * 8, (r - lo) % 8
                            picked = [
                                own_ref[z * 2 + half, base : base + 8].astype(jnp.float32)[down : down + 1]
                                for z in range(levs)
                            ]
                            rows_ref[i, k, :, lane : lane + lanes] = jnp.concatenate(picked, axis=0)[
                                :, at_lane : at_lane + lanes
                            ].astype(rows_ref.dtype)


def pick(own, levs, rows):
    vmem = pl.BlockSpec(memory_space=pltpu.VMEM)
    return pl.pallas_call(
        functools.partial(pick_kernel, rows),
        out_shape=(
            jax.ShapeDtypeStruct((2, FIELDS, levs, (FULL + 1) * LANES), own.dtype),
            jax.ShapeDtypeStruct(own.shape, own.dtype),
        ),
        in_specs=[vmem],
        out_specs=(vmem, vmem),
        compiler_params=pltpu.CompilerParams(vmem_limit_bytes=VMEM_LIMIT),
        name="pick",
    )(own)


def rows_kernel(
    q_ref, far_ref, near_ref, mask_ref, own_ref, other_ref,
    to_far_ref, to_near_ref, field_ref, south_ref, north_ref,
):
    vecs, levs, rows, lon = q_ref.shape
    lev = lax.broadcasted_iota(jnp.int32, (levs, lon), 0)
    own_column, odd = this_column(), odd_band()
    set_halos(near_ref, far_ref, south_ref, north_ref)

    def row_of(v, r):
        return jnp.concatenate([q_ref[v, z, r : r + 1] for z in range(levs)], axis=0)

    for i, r, step in ((0, 0, 1), (1, rows - 1, -1)):
        for own in range(COLUMNS):

            @pl.when(own_column == own)
            def _():
                for half in range(2):
                    for k, lane, lanes, lo, hi, column, _, _ in field_parts(rows, half):
                        if lo <= r < hi:
                            picked_ref = own_ref if column == own else other_ref
                            field_ref[k, :, lane : lane + lanes] = picked_ref[i, k, :, lane : lane + lanes].astype(
                                jnp.float32
                            )

        weight = weights(*(field_ref[k, :, :lon] for k in range(FIELDS)), mask_ref[r : r + 1].astype(jnp.float32))
        new = []
        for v in range(vecs):
            c, inner = row_of(v, r), row_of(v, r + step)
            n, s = (inner, south_ref[v]) if r == 0 else (north_ref[v], inner)
            u = jnp.where(lev == 0, c, pltpu.roll(c, 1, 0))
            b = jnp.where(lev == levs - 1, c, pltpu.roll(c, levs - 1, 0))
            new.append(advance(c, n, s, u, b, weight))

        @pl.when(odd == (1 if r == 0 else 0))
        def _():
            for v in range(vecs):
                to_near_ref[v] = new[v]

        @pl.when(odd == (0 if r == 0 else 1))
        def _():
            for v in range(vecs):
                to_far_ref[v] = new[v]


def hour_kernel(
    q_ref, far_ref, near_ref, mask_ref, own_ref, other_ref,
    out_ref, field_ref, south_ref, north_ref, new_ref=None, sent=None,
):
    vecs, levs, rows, lon = q_ref.shape
    row = lax.broadcasted_iota(jnp.int32, (rows, lon), 0)
    mask = mask_ref[...].astype(jnp.float32)
    own_column = this_column()
    set_halos(near_ref, far_ref, south_ref, north_ref)
    to_ref = out_ref if new_ref is None else new_ref

    def sending(level):
        return pltpu.make_async_copy(new_ref.at[:, level], out_ref.at[:, level], sent.at[level])

    def step(level):
        weight = weights(*(field_ref[k, :, :lon] for k in range(FIELDS)), mask)
        up, low = max(level - 1, 0), min(level + 1, levs - 1)
        for v in range(vecs):
            c = q_ref[v, level]
            n = jnp.where(row == rows - 1, north_ref[v, level : level + 1], pltpu.roll(c, rows - 1, 0))
            s = jnp.where(row == 0, south_ref[v, level : level + 1], pltpu.roll(c, 1, 0))
            to_ref[v, level] = advance(c, n, s, q_ref[v, up], q_ref[v, low], weight)
        if new_ref is not None:
            sending(level).start()

    for own in range(COLUMNS):

        @pl.when(own_column == own)
        def _():
            for level in range(levs):
                for half in range(2):
                    for k, lane, lanes, lo, hi, column, at, at_lane in field_parts(rows, half):
                        piece_ref = own_ref if column == own else other_ref
                        part = piece_ref[level * 2 + half, at : at + hi - lo].astype(jnp.float32)
                        field_ref[k, lo:hi, lane : lane + lanes] = part[:, at_lane : at_lane + lanes]
                step(level)

    if new_ref is not None:
        for level in range(levs):
            sending(level).wait()


def on_band(kernel, name, outs, out_space, field_rows, flops, args, scratch=()):
    vmem = pl.BlockSpec(memory_space=pltpu.VMEM)
    lon = args[0].shape[-1]
    bytes_accessed = sum(a.size * a.dtype.itemsize for a in (*args, *outs))
    return pl.pallas_call(
        kernel,
        out_shape=outs,
        in_specs=[vmem] * len(args),
        out_specs=tuple(pl.BlockSpec(memory_space=out_space) for _ in outs),
        scratch_shapes=[
            pltpu.VMEM((FIELDS, field_rows, -(-lon // LANES) * LANES), jnp.float32),
            pltpu.VMEM(args[1].shape, jnp.float32),
            pltpu.VMEM(args[1].shape, jnp.float32),
            *scratch,
        ],
        compiler_params=pltpu.CompilerParams(vmem_limit_bytes=VMEM_LIMIT),
        cost_estimate=pl.CostEstimate(flops=flops, bytes_accessed=bytes_accessed, transcendentals=0),
        name=name,
    )(*args)


def edge_rows(*args):
    vecs, levs, _, lon = args[0].shape
    edge = jax.ShapeDtypeStruct((vecs, levs, lon), jnp.float32)
    return on_band(rows_kernel, "edge_rows", (edge, edge), pltpu.VMEM, levs, 30 * edge.size, args)


def one_hour(*args):
    q = args[0]
    out = jax.ShapeDtypeStruct(q.shape, q.dtype)
    return on_band(hour_kernel, "one_hour", (out,), pltpu.VMEM, q.shape[2], 20 * q.size, args)[0]


def last_hour(*args):
    q = args[0]
    out = jax.ShapeDtypeStruct(q.shape, q.dtype)
    scratch = (pltpu.VMEM(q.shape, q.dtype), pltpu.SemaphoreType.DMA((q.shape[1],)))
    return on_band(hour_kernel, "last_hour", (out,), pl.ANY, q.shape[2], 20 * q.size, args, scratch)[0]


def shards(perturb, trajectory, hour_slot, sea_mask):
    lat = lax.axis_size("lat")
    column = this_column()
    odd = odd_band()
    on_chip = [(i, i ^ 1) for i in range(lat)]
    between = [pair for i in range(1, lat - 1, 2) for pair in ((i, i + 1), (i + 1, i))]
    rings = [[c * RING + z for z in range(RING)] for c in range(COLUMNS)]
    swap = [(i, (i + RING) % (COLUMNS * RING)) for i in range(COLUMNS * RING)]

    def halos(to_far, to_near):
        far = lax.ppermute(to_far, "lat", between)
        return far, lax.ppermute(to_near, "lat", on_chip)

    first, last = perturb[:, :, 0], perturb[:, :, -1]
    halo = halos(jnp.where(odd == 1, last, first), jnp.where(odd == 1, first, last))

    end, last_slot = RING - 1, COLUMNS * RING - 1
    keep, send = pack(trajectory)
    crossed = lax.ppermute(send, "vec", swap)
    moved = lax.ppermute(keep, "vec", [(c * RING + end, c * RING + end - 1) for c in range(COLUMNS)])
    asked = hour_slot[0] + hour_slot[1] - last_slot
    both = asked == end
    z = lax.axis_index("vec") % RING
    own_there = jnp.where(z == end, (column == 1) & ~both, asked // RING == column)
    offered = jnp.where((z == end - 1) & both, moved, jnp.where(own_there, keep, crossed))
    place = jnp.where(both & (hour_slot // RING == column), end - 1, hour_slot % RING)

    pieces = lax.all_to_all(offered, "vec", 0, 0, axis_index_groups=rings, tiled=True)
    picked = jnp.stack([lax.dynamic_index_in_dim(pieces, place[h], 0, keepdims=False) for h in range(2)])
    picked = picked + (sum(h[0, 0, 0] for h in halo) * 0).astype(picked.dtype)
    gathered = lax.all_gather(picked, "vec", axis=0, axis_index_groups=rings)
    own = [gathered[:, h] for h in range(2)]
    own_rows, half = pick(own[0], perturb.shape[1], perturb.shape[2])
    other_rows = lax.ppermute(own_rows, "vec", swap)
    late = jnp.where(column == 0, other_rows[0, 0, 0, 2 * LANES], other_rows[0, 0, 0, 0]) * 0
    other = [lax.ppermute(half, "vec", swap), lax.ppermute(own[1] + late, "vec", swap)]

    next_halo = halos(*edge_rows(perturb, *halo, sea_mask, own_rows, other_rows))
    q = one_hour(perturb, *halo, sea_mask, own[0], other[0])
    return last_hour(q, *next_halo, sea_mask, own[1], other[1])


def solution(mesh):
    return jax.shard_map(
        shards,
        mesh=mesh,
        in_specs=(
            P("vec", None, "lat", None),
            P("vec", None, None, "lat", None),
            P(),
            P("lat", None),
        ),
        out_specs=P("vec", None, "lat", None),
        check_vma=False,
    )
```

```python
import jax
import jax.numpy as jnp
from jax import lax
from jax.experimental import pallas as pl
from jax.experimental.pallas import tpu as pltpu
from jax.sharding import PartitionSpec as P

COLUMNS = 2
RING = 16
LANES = 128
FIELDS = 3
FULL = 5
TALL = 40
PIECE = 104
VMEM_LIMIT = 48 * 1024 * 1024


def this_column():
    return lax.axis_index("vec") // RING


def odd_band():
    return lax.axis_index("lat") % 2


def level_parts(rows):
    total = FIELDS * rows
    parts = [(t * LANES, LANES, 0, total, t * total, 0) for t in range(FULL)]
    lane, at = FULL * LANES, FULL * total
    parts.append((lane, 64, 0, TALL, at, 0))
    parts.append((lane, 64, TALL, total, at, 64))
    lane, at = lane + 64, at + TALL
    for start in range(0, total, 8):
        down, across = divmod(start // 8, 8)
        parts.append((lane, 16, start, start + 8, at + 8 * down, 16 * across))
    return parts


def field_parts(rows, half):
    parts = []
    for lane, lanes, start, stop, at, at_lane in level_parts(rows):
        for k in range(FIELDS):
            for column in range(COLUMNS):
                top = (half * COLUMNS + column) * PIECE
                lo = max(start, k * rows, start + top - at)
                hi = min(stop, (k + 1) * rows, start + top + PIECE - at)
                if lo < hi:
                    parts.append((k, lane, lanes, lo - k * rows, hi - k * rows, column, at + lo - start - top, at_lane))
    return parts


def pack_kernel(field_ref, keep_ref, send_ref):
    _, levs, rows, lon = field_ref.shape[1:]
    for own in range(COLUMNS):

        @pl.when(this_column() == own)
        def _():
            for level in range(levs):
                for half in range(2):
                    for k, lane, lanes, lo, hi, column, at, at_lane in field_parts(rows, half):
                        piece_ref = keep_ref if column == own else send_ref
                        piece_ref[level * 2 + half, at : at + hi - lo, at_lane : at_lane + lanes] = field_ref[
                            0, k, level, lo:hi, lane : lane + lanes
                        ]


def pack(trajectory):
    half = jax.ShapeDtypeStruct((RING, PIECE, LANES), trajectory.dtype)
    vmem = pl.BlockSpec(memory_space=pltpu.VMEM)
    return pl.pallas_call(
        pack_kernel,
        out_shape=(half, half),
        in_specs=[vmem],
        out_specs=(vmem, vmem),
        compiler_params=pltpu.CompilerParams(vmem_limit_bytes=VMEM_LIMIT),
        name="pack",
    )(trajectory)


def lanes_next(x):
    return jnp.concatenate([x[..., 1:], x[..., :1]], axis=-1)


def lanes_prev(x):
    return jnp.concatenate([x[..., -1:], x[..., :-1]], axis=-1)


def weights(f0, f1, f2, mask):
    diffuse = mask * (0.06 + 0.015 * f0)
    zonal, merid = mask * (0.15 * f1), mask * (0.15 * f2)
    return (
        0.8 * mask - 4.0 * diffuse,
        diffuse - zonal,
        diffuse + zonal,
        diffuse - merid,
        diffuse + merid,
        0.1 * mask,
    )


def advance(c, n, s, u, b, weight):
    wc, we, ww, wn, ws, wl = weight
    return (wc * c + we * lanes_next(c) + ww * lanes_prev(c)) + (wn * n + ws * s + wl * (u + b))


def set_halos(near_ref, far_ref, south_ref, north_ref):
    @pl.when(odd_band() == 1)
    def _():
        south_ref[...] = near_ref[...]
        north_ref[...] = far_ref[...]

    @pl.when(odd_band() == 0)
    def _():
        south_ref[...] = far_ref[...]
        north_ref[...] = near_ref[...]


def rows_kernel(
    q_ref, far_ref, near_ref, mask_ref, own_ref, other_ref,
    to_far_ref, to_near_ref, field_ref, south_ref, north_ref,
):
    vecs, levs, rows, lon = q_ref.shape
    lev = lax.broadcasted_iota(jnp.int32, (levs, lon), 0)
    own_column, odd = this_column(), odd_band()
    set_halos(near_ref, far_ref, south_ref, north_ref)

    def row_of(v, r):
        return jnp.concatenate([q_ref[v, z, r : r + 1] for z in range(levs)], axis=0)

    for r, step in ((0, 1), (rows - 1, -1)):
        for own in range(COLUMNS):

            @pl.when(own_column == own)
            def _():
                for half in range(2):
                    for k, lane, lanes, lo, hi, column, at, at_lane in field_parts(rows, half):
                        if lo <= r < hi:
                            piece_ref = own_ref if column == own else other_ref
                            base = at + (r - lo) // 8 * 8
                            for z in range(levs):
                                eight = piece_ref[z * 2 + half, base : base + 8].astype(jnp.float32)
                                i = (r - lo) % 8
                                field_ref[k, z : z + 1, lane : lane + lanes] = eight[
                                    i : i + 1, at_lane : at_lane + lanes
                                ]

        weight = weights(*(field_ref[k, :, :lon] for k in range(FIELDS)), mask_ref[r : r + 1].astype(jnp.float32))
        new = []
        for v in range(vecs):
            c, inner = row_of(v, r), row_of(v, r + step)
            n, s = (inner, south_ref[v]) if r == 0 else (north_ref[v], inner)
            u = jnp.where(lev == 0, c, pltpu.roll(c, 1, 0))
            b = jnp.where(lev == levs - 1, c, pltpu.roll(c, levs - 1, 0))
            new.append(advance(c, n, s, u, b, weight))

        @pl.when(odd == (1 if r == 0 else 0))
        def _():
            for v in range(vecs):
                to_near_ref[v] = new[v]

        @pl.when(odd == (0 if r == 0 else 1))
        def _():
            for v in range(vecs):
                to_far_ref[v] = new[v]


def hour_kernel(
    q_ref, far_ref, near_ref, mask_ref, own_ref, other_ref,
    out_ref, field_ref, south_ref, north_ref, new_ref=None, sent=None,
):
    vecs, levs, rows, lon = q_ref.shape
    row = lax.broadcasted_iota(jnp.int32, (rows, lon), 0)
    mask = mask_ref[...].astype(jnp.float32)
    own_column = this_column()
    set_halos(near_ref, far_ref, south_ref, north_ref)
    to_ref = out_ref if new_ref is None else new_ref

    def sending(level):
        return pltpu.make_async_copy(new_ref.at[:, level], out_ref.at[:, level], sent.at[level])

    def step(level):
        weight = weights(*(field_ref[k, :, :lon] for k in range(FIELDS)), mask)
        up, low = max(level - 1, 0), min(level + 1, levs - 1)
        for v in range(vecs):
            c = q_ref[v, level]
            n = jnp.where(row == rows - 1, north_ref[v, level : level + 1], pltpu.roll(c, rows - 1, 0))
            s = jnp.where(row == 0, south_ref[v, level : level + 1], pltpu.roll(c, 1, 0))
            to_ref[v, level] = advance(c, n, s, q_ref[v, up], q_ref[v, low], weight)
        if new_ref is not None:
            sending(level).start()

    for own in range(COLUMNS):

        @pl.when(own_column == own)
        def _():
            for level in range(levs):
                for half in range(2):
                    for k, lane, lanes, lo, hi, column, at, at_lane in field_parts(rows, half):
                        piece_ref = own_ref if column == own else other_ref
                        part = piece_ref[level * 2 + half, at : at + hi - lo].astype(jnp.float32)
                        field_ref[k, lo:hi, lane : lane + lanes] = part[:, at_lane : at_lane + lanes]
                step(level)

    if new_ref is not None:
        for level in range(levs):
            sending(level).wait()


def on_band(kernel, name, outs, out_space, field_rows, flops, args, scratch=()):
    vmem = pl.BlockSpec(memory_space=pltpu.VMEM)
    lon = args[0].shape[-1]
    bytes_accessed = sum(a.size * a.dtype.itemsize for a in (*args, *outs))
    return pl.pallas_call(
        kernel,
        out_shape=outs,
        in_specs=[vmem] * len(args),
        out_specs=tuple(pl.BlockSpec(memory_space=out_space) for _ in outs),
        scratch_shapes=[
            pltpu.VMEM((FIELDS, field_rows, -(-lon // LANES) * LANES), jnp.float32),
            pltpu.VMEM(args[1].shape, jnp.float32),
            pltpu.VMEM(args[1].shape, jnp.float32),
            *scratch,
        ],
        compiler_params=pltpu.CompilerParams(vmem_limit_bytes=VMEM_LIMIT),
        cost_estimate=pl.CostEstimate(flops=flops, bytes_accessed=bytes_accessed, transcendentals=0),
        name=name,
    )(*args)


def edge_rows(*args):
    vecs, levs, _, lon = args[0].shape
    edge = jax.ShapeDtypeStruct((vecs, levs, lon), jnp.float32)
    return on_band(rows_kernel, "edge_rows", (edge, edge), pltpu.VMEM, levs, 30 * edge.size, args)


def one_hour(*args):
    q = args[0]
    out = jax.ShapeDtypeStruct(q.shape, q.dtype)
    return on_band(hour_kernel, "one_hour", (out,), pltpu.VMEM, q.shape[2], 20 * q.size, args)[0]


def last_hour(*args):
    q = args[0]
    out = jax.ShapeDtypeStruct(q.shape, q.dtype)
    scratch = (pltpu.VMEM(q.shape, q.dtype), pltpu.SemaphoreType.DMA((q.shape[1],)))
    return on_band(hour_kernel, "last_hour", (out,), pl.ANY, q.shape[2], 20 * q.size, args, scratch)[0]


def shards(perturb, trajectory, hour_slot, sea_mask):
    lat = lax.axis_size("lat")
    column = this_column()
    odd = odd_band()
    on_chip = [(i, i ^ 1) for i in range(lat)]
    between = [pair for i in range(1, lat - 1, 2) for pair in ((i, i + 1), (i + 1, i))]
    rings = [[c * RING + z for z in range(RING)] for c in range(COLUMNS)]
    swap = [(i, (i + RING) % (COLUMNS * RING)) for i in range(COLUMNS * RING)]

    def halos(to_far, to_near):
        far = lax.ppermute(to_far, "lat", between)
        return far, lax.ppermute(to_near, "lat", on_chip)

    first, last = perturb[:, :, 0], perturb[:, :, -1]
    halo = halos(jnp.where(odd == 1, last, first), jnp.where(odd == 1, first, last))

    end, last_slot = RING - 1, COLUMNS * RING - 1
    keep, send = pack(trajectory)
    crossed = lax.ppermute(send, "vec", swap)
    moved = lax.ppermute(keep, "vec", [(c * RING + end, c * RING + end - 1) for c in range(COLUMNS)])
    asked = hour_slot[0] + hour_slot[1] - last_slot
    both = asked == end
    z = lax.axis_index("vec") % RING
    own_there = jnp.where(z == end, (column == 1) & ~both, asked // RING == column)
    offered = jnp.where((z == end - 1) & both, moved, jnp.where(own_there, keep, crossed))
    place = jnp.where(both & (hour_slot // RING == column), end - 1, hour_slot % RING)

    pieces = lax.all_to_all(offered, "vec", 0, 0, axis_index_groups=rings, tiled=True)
    picked = jnp.stack([lax.dynamic_index_in_dim(pieces, place[h], 0, keepdims=False) for h in range(2)])
    picked = picked + (sum(h[0, 0, 0] for h in halo) * 0).astype(picked.dtype)
    gathered = lax.all_gather(picked, "vec", axis=0, axis_index_groups=rings)
    own = [gathered[:, h] for h in range(2)]
    other = [lax.ppermute(half, "vec", swap) for half in own]

    args = (perturb, *halo, sea_mask, own[0], other[0])
    halo = halos(*edge_rows(*args))
    return last_hour(one_hour(*args), *halo, sea_mask, own[1], other[1])


def solution(mesh):
    return jax.shard_map(
        shards,
        mesh=mesh,
        in_specs=(
            P("vec", None, "lat", None),
            P("vec", None, None, "lat", None),
            P(),
            P("lat", None),
        ),
        out_specs=P("vec", None, "lat", None),
        check_vma=False,
    )
```

```python
import jax
import jax.numpy as jnp
from jax import lax
from jax.experimental import pallas as pl
from jax.experimental.pallas import tpu as pltpu
from jax.sharding import PartitionSpec as P

COLUMNS = 2
RING = 16
LANES = 128
FIELDS = 3
FULL = 5
TALL = 40
PIECE = 104
VMEM_LIMIT = 48 * 1024 * 1024


def this_column():
    return lax.axis_index("vec") // RING


def odd_band():
    return lax.axis_index("lat") % 2


def level_parts(rows):
    total = FIELDS * rows
    parts = [(t * LANES, LANES, 0, total, t * total, 0) for t in range(FULL)]
    lane, at = FULL * LANES, FULL * total
    parts.append((lane, 64, 0, TALL, at, 0))
    parts.append((lane, 64, TALL, total, at, 64))
    lane, at = lane + 64, at + TALL
    for start in range(0, total, 8):
        down, across = divmod(start // 8, 8)
        parts.append((lane, 16, start, start + 8, at + 8 * down, 16 * across))
    return parts


def field_parts(rows, half):
    parts = []
    for lane, lanes, start, stop, at, at_lane in level_parts(rows):
        for k in range(FIELDS):
            for column in range(COLUMNS):
                top = (half * COLUMNS + column) * PIECE
                lo = max(start, k * rows, start + top - at)
                hi = min(stop, (k + 1) * rows, start + top + PIECE - at)
                if lo < hi:
                    parts.append((k, lane, lanes, lo - k * rows, hi - k * rows, column, at + lo - start - top, at_lane))
    return parts


def pack_kernel(field_ref, keep_ref, send_ref):
    _, levs, rows, lon = field_ref.shape[1:]
    for own in range(COLUMNS):

        @pl.when(this_column() == own)
        def _():
            for level in range(levs):
                for half in range(2):
                    for k, lane, lanes, lo, hi, column, at, at_lane in field_parts(rows, half):
                        piece_ref = keep_ref if column == own else send_ref
                        piece_ref[level * 2 + half, at : at + hi - lo, at_lane : at_lane + lanes] = field_ref[
                            0, k, level, lo:hi, lane : lane + lanes
                        ]


def pack(trajectory):
    half = jax.ShapeDtypeStruct((RING, PIECE, LANES), trajectory.dtype)
    vmem = pl.BlockSpec(memory_space=pltpu.VMEM)
    return pl.pallas_call(
        pack_kernel,
        out_shape=(half, half),
        in_specs=[vmem],
        out_specs=(vmem, vmem),
        compiler_params=pltpu.CompilerParams(vmem_limit_bytes=VMEM_LIMIT),
        name="pack",
    )(trajectory)


def offer_kernel(choice_ref, keep_ref, crossed_ref, moved_ref, offered_ref, done):
    for i, ref in enumerate((keep_ref, crossed_ref, moved_ref)):

        @pl.when(choice_ref[0] == i)
        def _():
            copy = pltpu.make_async_copy(ref, offered_ref, done)
            copy.start()
            copy.wait()


def offer(choice, *halves):
    anywhere = pl.BlockSpec(memory_space=pl.ANY)
    return pl.pallas_call(
        offer_kernel,
        out_shape=jax.ShapeDtypeStruct(halves[0].shape, halves[0].dtype),
        in_specs=[pl.BlockSpec(memory_space=pltpu.SMEM)] + [anywhere] * len(halves),
        out_specs=anywhere,
        scratch_shapes=[pltpu.SemaphoreType.DMA],
        compiler_params=pltpu.CompilerParams(vmem_limit_bytes=VMEM_LIMIT),
        name="offer",
    )(choice, *halves)


def lanes_next(x):
    return jnp.concatenate([x[..., 1:], x[..., :1]], axis=-1)


def lanes_prev(x):
    return jnp.concatenate([x[..., -1:], x[..., :-1]], axis=-1)


def weights(f0, f1, f2, mask):
    diffuse = mask * (0.06 + 0.015 * f0)
    zonal, merid = mask * (0.15 * f1), mask * (0.15 * f2)
    return (
        0.8 * mask - 4.0 * diffuse,
        diffuse - zonal,
        diffuse + zonal,
        diffuse - merid,
        diffuse + merid,
        0.1 * mask,
    )


def advance(c, n, s, u, b, weight):
    wc, we, ww, wn, ws, wl = weight
    return (wc * c + we * lanes_next(c) + ww * lanes_prev(c)) + (wn * n + ws * s + wl * (u + b))


def set_halos(near_ref, far_ref, south_ref, north_ref):
    @pl.when(odd_band() == 1)
    def _():
        south_ref[...] = near_ref[...]
        north_ref[...] = far_ref[...]

    @pl.when(odd_band() == 0)
    def _():
        south_ref[...] = far_ref[...]
        north_ref[...] = near_ref[...]


def rows_kernel(
    q_ref, far_ref, near_ref, mask_ref, own_ref, other_ref,
    to_far_ref, to_near_ref, field_ref, south_ref, north_ref,
):
    vecs, levs, rows, lon = q_ref.shape
    lev = lax.broadcasted_iota(jnp.int32, (levs, lon), 0)
    own_column, odd = this_column(), odd_band()
    set_halos(near_ref, far_ref, south_ref, north_ref)

    def row_of(v, r):
        return jnp.concatenate([q_ref[v, z, r : r + 1] for z in range(levs)], axis=0)

    for r, step in ((0, 1), (rows - 1, -1)):
        for own in range(COLUMNS):

            @pl.when(own_column == own)
            def _():
                for half in range(2):
                    for k, lane, lanes, lo, hi, column, at, at_lane in field_parts(rows, half):
                        if lo <= r < hi:
                            piece_ref = own_ref if column == own else other_ref
                            base = at + (r - lo) // 8 * 8
                            for z in range(levs):
                                eight = piece_ref[z * 2 + half, base : base + 8].astype(jnp.float32)
                                i = (r - lo) % 8
                                field_ref[k, z : z + 1, lane : lane + lanes] = eight[
                                    i : i + 1, at_lane : at_lane + lanes
                                ]

        weight = weights(*(field_ref[k, :, :lon] for k in range(FIELDS)), mask_ref[r : r + 1].astype(jnp.float32))
        new = []
        for v in range(vecs):
            c, inner = row_of(v, r), row_of(v, r + step)
            n, s = (inner, south_ref[v]) if r == 0 else (north_ref[v], inner)
            u = jnp.where(lev == 0, c, pltpu.roll(c, 1, 0))
            b = jnp.where(lev == levs - 1, c, pltpu.roll(c, levs - 1, 0))
            new.append(advance(c, n, s, u, b, weight))

        @pl.when(odd == (1 if r == 0 else 0))
        def _():
            for v in range(vecs):
                to_near_ref[v] = new[v]

        @pl.when(odd == (0 if r == 0 else 1))
        def _():
            for v in range(vecs):
                to_far_ref[v] = new[v]


def hour_kernel(
    q_ref, far_ref, near_ref, mask_ref, own_ref, other_ref,
    out_ref, field_ref, south_ref, north_ref, new_ref=None, sent=None,
):
    vecs, levs, rows, lon = q_ref.shape
    row = lax.broadcasted_iota(jnp.int32, (rows, lon), 0)
    mask = mask_ref[...].astype(jnp.float32)
    own_column = this_column()
    set_halos(near_ref, far_ref, south_ref, north_ref)
    to_ref = out_ref if new_ref is None else new_ref

    def sending(level):
        return pltpu.make_async_copy(new_ref.at[:, level], out_ref.at[:, level], sent.at[level])

    def step(level):
        weight = weights(*(field_ref[k, :, :lon] for k in range(FIELDS)), mask)
        up, low = max(level - 1, 0), min(level + 1, levs - 1)
        for v in range(vecs):
            c = q_ref[v, level]
            n = jnp.where(row == rows - 1, north_ref[v, level : level + 1], pltpu.roll(c, rows - 1, 0))
            s = jnp.where(row == 0, south_ref[v, level : level + 1], pltpu.roll(c, 1, 0))
            to_ref[v, level] = advance(c, n, s, q_ref[v, up], q_ref[v, low], weight)
        if new_ref is not None:
            sending(level).start()

    for own in range(COLUMNS):

        @pl.when(own_column == own)
        def _():
            for level in range(levs):
                for half in range(2):
                    for k, lane, lanes, lo, hi, column, at, at_lane in field_parts(rows, half):
                        piece_ref = own_ref if column == own else other_ref
                        part = piece_ref[level * 2 + half, at : at + hi - lo].astype(jnp.float32)
                        field_ref[k, lo:hi, lane : lane + lanes] = part[:, at_lane : at_lane + lanes]
                step(level)

    if new_ref is not None:
        for level in range(levs):
            sending(level).wait()


def on_band(kernel, name, outs, out_space, field_rows, flops, args, scratch=()):
    vmem = pl.BlockSpec(memory_space=pltpu.VMEM)
    lon = args[0].shape[-1]
    bytes_accessed = sum(a.size * a.dtype.itemsize for a in (*args, *outs))
    return pl.pallas_call(
        kernel,
        out_shape=outs,
        in_specs=[vmem] * len(args),
        out_specs=tuple(pl.BlockSpec(memory_space=out_space) for _ in outs),
        scratch_shapes=[
            pltpu.VMEM((FIELDS, field_rows, -(-lon // LANES) * LANES), jnp.float32),
            pltpu.VMEM(args[1].shape, jnp.float32),
            pltpu.VMEM(args[1].shape, jnp.float32),
            *scratch,
        ],
        compiler_params=pltpu.CompilerParams(vmem_limit_bytes=VMEM_LIMIT),
        cost_estimate=pl.CostEstimate(flops=flops, bytes_accessed=bytes_accessed, transcendentals=0),
        name=name,
    )(*args)


def edge_rows(*args):
    vecs, levs, _, lon = args[0].shape
    edge = jax.ShapeDtypeStruct((vecs, levs, lon), jnp.float32)
    return on_band(rows_kernel, "edge_rows", (edge, edge), pltpu.VMEM, levs, 30 * edge.size, args)


def one_hour(*args):
    q = args[0]
    out = jax.ShapeDtypeStruct(q.shape, q.dtype)
    return on_band(hour_kernel, "one_hour", (out,), pltpu.VMEM, q.shape[2], 20 * q.size, args)[0]


def last_hour(*args):
    q = args[0]
    out = jax.ShapeDtypeStruct(q.shape, q.dtype)
    scratch = (pltpu.VMEM(q.shape, q.dtype), pltpu.SemaphoreType.DMA((q.shape[1],)))
    return on_band(hour_kernel, "last_hour", (out,), pl.ANY, q.shape[2], 20 * q.size, args, scratch)[0]


def shards(perturb, trajectory, hour_slot, sea_mask):
    lat = lax.axis_size("lat")
    column = this_column()
    odd = odd_band()
    on_chip = [(i, i ^ 1) for i in range(lat)]
    between = [pair for i in range(1, lat - 1, 2) for pair in ((i, i + 1), (i + 1, i))]
    rings = [[c * RING + z for z in range(RING)] for c in range(COLUMNS)]
    swap = [(i, (i + RING) % (COLUMNS * RING)) for i in range(COLUMNS * RING)]

    def halos(to_far, to_near):
        far = lax.ppermute(to_far, "lat", between)
        return far, lax.ppermute(to_near, "lat", on_chip)

    first, last = perturb[:, :, 0], perturb[:, :, -1]
    halo = halos(jnp.where(odd == 1, last, first), jnp.where(odd == 1, first, last))

    end, last_slot = RING - 1, COLUMNS * RING - 1
    keep, send = pack(trajectory)
    crossed = lax.ppermute(send, "vec", swap)
    moved = lax.ppermute(keep, "vec", [(c * RING + end, c * RING + end - 1) for c in range(COLUMNS)])
    asked = hour_slot[0] + hour_slot[1] - last_slot
    both = asked == end
    z = lax.axis_index("vec") % RING
    own_there = jnp.where(z == end, (column == 1) & ~both, asked // RING == column)
    choice = jnp.where((z == end - 1) & both, 2, jnp.where(own_there, 0, 1)).astype(jnp.int32)
    offered = offer(choice[None], keep, crossed, moved)
    place = jnp.where(both & (hour_slot // RING == column), end - 1, hour_slot % RING)

    pieces = lax.all_to_all(offered, "vec", 0, 0, axis_index_groups=rings, tiled=True)
    picked = jnp.stack([lax.dynamic_index_in_dim(pieces, place[h], 0, keepdims=False) for h in range(2)])
    picked = picked + (sum(h[0, 0, 0] for h in halo) * 0).astype(picked.dtype)
    gathered = lax.all_gather(picked, "vec", axis=0, axis_index_groups=rings)
    own = [gathered[:, h] for h in range(2)]
    other = [lax.ppermute(half, "vec", swap) for half in own]

    args = (perturb, *halo, sea_mask, own[0], other[0])
    halo = halos(*edge_rows(*args))
    return last_hour(one_hour(*args), *halo, sea_mask, own[1], other[1])


def solution(mesh):
    return jax.shard_map(
        shards,
        mesh=mesh,
        in_specs=(
            P("vec", None, "lat", None),
            P("vec", None, None, "lat", None),
            P(),
            P("lat", None),
        ),
        out_specs=P("vec", None, "lat", None),
        check_vma=False,
    )
```

```python
import jax
import jax.numpy as jnp
from jax import lax
from jax.experimental import pallas as pl
from jax.experimental.pallas import tpu as pltpu
from jax.sharding import PartitionSpec as P

COLUMNS = 2
RING = 16
LANES = 128
FIELDS = 3
FULL = 5
TALL = 40
PIECE = 104
VMEM_LIMIT = 48 * 1024 * 1024


def this_column():
    return lax.axis_index("vec") // RING


def odd_band():
    return lax.axis_index("lat") % 2


def level_parts(rows):
    total = FIELDS * rows
    parts = [(t * LANES, LANES, 0, total, t * total, 0) for t in range(FULL)]
    lane, at = FULL * LANES, FULL * total
    parts.append((lane, 64, 0, TALL, at, 0))
    parts.append((lane, 64, TALL, total, at, 64))
    lane, at = lane + 64, at + TALL
    for start in range(0, total, 8):
        down, across = divmod(start // 8, 8)
        parts.append((lane, 16, start, start + 8, at + 8 * down, 16 * across))
    return parts


def field_parts(rows, half):
    parts = []
    for lane, lanes, start, stop, at, at_lane in level_parts(rows):
        for k in range(FIELDS):
            for column in range(COLUMNS):
                top = (half * COLUMNS + column) * PIECE
                lo = max(start, k * rows, start + top - at)
                hi = min(stop, (k + 1) * rows, start + top + PIECE - at)
                if lo < hi:
                    parts.append((k, lane, lanes, lo - k * rows, hi - k * rows, column, at + lo - start - top, at_lane))
    return parts


def pack_kernel(stored_ref, keep_ref, send_ref, field_ref, landed):
    _, levs, rows, lon = stored_ref.shape[1:]

    def landing(level):
        return pltpu.make_async_copy(stored_ref.at[0, :, level], field_ref.at[:, level], landed.at[level])

    for level in range(levs):
        landing(level).start()
    for own in range(COLUMNS):

        @pl.when(this_column() == own)
        def _():
            for level in range(levs):
                landing(level).wait()
                for half in range(2):
                    for k, lane, lanes, lo, hi, column, at, at_lane in field_parts(rows, half):
                        piece_ref = keep_ref if column == own else send_ref
                        piece_ref[level * 2 + half, at : at + hi - lo, at_lane : at_lane + lanes] = field_ref[
                            k, level, lo:hi, lane : lane + lanes
                        ]


def pack(trajectory):
    half = jax.ShapeDtypeStruct((RING, PIECE, LANES), trajectory.dtype)
    vmem = pl.BlockSpec(memory_space=pltpu.VMEM)
    return pl.pallas_call(
        pack_kernel,
        out_shape=(half, half),
        in_specs=[pl.BlockSpec(memory_space=pl.ANY)],
        out_specs=(vmem, vmem),
        scratch_shapes=[
            pltpu.VMEM(trajectory.shape[1:], trajectory.dtype),
            pltpu.SemaphoreType.DMA((trajectory.shape[2],)),
        ],
        compiler_params=pltpu.CompilerParams(vmem_limit_bytes=VMEM_LIMIT),
        name="pack",
    )(trajectory)


def offer_kernel(choice_ref, keep_ref, crossed_ref, moved_ref, offered_ref, done):
    for i, ref in enumerate((keep_ref, crossed_ref, moved_ref)):

        @pl.when(choice_ref[0] == i)
        def _():
            copy = pltpu.make_async_copy(ref, offered_ref, done)
            copy.start()
            copy.wait()


def offer(choice, *halves):
    anywhere = pl.BlockSpec(memory_space=pl.ANY)
    return pl.pallas_call(
        offer_kernel,
        out_shape=jax.ShapeDtypeStruct(halves[0].shape, halves[0].dtype),
        in_specs=[pl.BlockSpec(memory_space=pltpu.SMEM)] + [anywhere] * len(halves),
        out_specs=anywhere,
        scratch_shapes=[pltpu.SemaphoreType.DMA],
        compiler_params=pltpu.CompilerParams(vmem_limit_bytes=VMEM_LIMIT),
        name="offer",
    )(choice, *halves)


def lanes_next(x):
    return jnp.concatenate([x[..., 1:], x[..., :1]], axis=-1)


def lanes_prev(x):
    return jnp.concatenate([x[..., -1:], x[..., :-1]], axis=-1)


def weights(f0, f1, f2, mask):
    diffuse = mask * (0.06 + 0.015 * f0)
    zonal, merid = mask * (0.15 * f1), mask * (0.15 * f2)
    return (
        0.8 * mask - 4.0 * diffuse,
        diffuse - zonal,
        diffuse + zonal,
        diffuse - merid,
        diffuse + merid,
        0.1 * mask,
    )


def advance(c, n, s, u, b, weight):
    wc, we, ww, wn, ws, wl = weight
    return (wc * c + we * lanes_next(c) + ww * lanes_prev(c)) + (wn * n + ws * s + wl * (u + b))


def set_halos(near_ref, far_ref, south_ref, north_ref):
    @pl.when(odd_band() == 1)
    def _():
        south_ref[...] = near_ref[...]
        north_ref[...] = far_ref[...]

    @pl.when(odd_band() == 0)
    def _():
        south_ref[...] = far_ref[...]
        north_ref[...] = near_ref[...]


def rows_kernel(
    q_ref, far_ref, near_ref, mask_ref, own_ref, other_ref,
    to_far_ref, to_near_ref, field_ref, south_ref, north_ref,
):
    vecs, levs, rows, lon = q_ref.shape
    lev = lax.broadcasted_iota(jnp.int32, (levs, lon), 0)
    own_column, odd = this_column(), odd_band()
    set_halos(near_ref, far_ref, south_ref, north_ref)

    def row_of(v, r):
        return jnp.concatenate([q_ref[v, z, r : r + 1] for z in range(levs)], axis=0)

    for r, step in ((0, 1), (rows - 1, -1)):
        for own in range(COLUMNS):

            @pl.when(own_column == own)
            def _():
                for half in range(2):
                    for k, lane, lanes, lo, hi, column, at, at_lane in field_parts(rows, half):
                        if lo <= r < hi:
                            piece_ref = own_ref if column == own else other_ref
                            base = at + (r - lo) // 8 * 8
                            for z in range(levs):
                                eight = piece_ref[z * 2 + half, base : base + 8].astype(jnp.float32)
                                i = (r - lo) % 8
                                field_ref[k, z : z + 1, lane : lane + lanes] = eight[
                                    i : i + 1, at_lane : at_lane + lanes
                                ]

        weight = weights(*(field_ref[k, :, :lon] for k in range(FIELDS)), mask_ref[r : r + 1].astype(jnp.float32))
        new = []
        for v in range(vecs):
            c, inner = row_of(v, r), row_of(v, r + step)
            n, s = (inner, south_ref[v]) if r == 0 else (north_ref[v], inner)
            u = jnp.where(lev == 0, c, pltpu.roll(c, 1, 0))
            b = jnp.where(lev == levs - 1, c, pltpu.roll(c, levs - 1, 0))
            new.append(advance(c, n, s, u, b, weight))

        @pl.when(odd == (1 if r == 0 else 0))
        def _():
            for v in range(vecs):
                to_near_ref[v] = new[v]

        @pl.when(odd == (0 if r == 0 else 1))
        def _():
            for v in range(vecs):
                to_far_ref[v] = new[v]


def hour_kernel(
    q_ref, far_ref, near_ref, mask_ref, own_ref, other_ref,
    out_ref, field_ref, south_ref, north_ref, new_ref=None, sent=None,
):
    vecs, levs, rows, lon = q_ref.shape
    row = lax.broadcasted_iota(jnp.int32, (rows, lon), 0)
    mask = mask_ref[...].astype(jnp.float32)
    own_column = this_column()
    set_halos(near_ref, far_ref, south_ref, north_ref)
    to_ref = out_ref if new_ref is None else new_ref

    def sending(level):
        return pltpu.make_async_copy(new_ref.at[:, level], out_ref.at[:, level], sent.at[level])

    def step(level):
        weight = weights(*(field_ref[k, :, :lon] for k in range(FIELDS)), mask)
        up, low = max(level - 1, 0), min(level + 1, levs - 1)
        for v in range(vecs):
            c = q_ref[v, level]
            n = jnp.where(row == rows - 1, north_ref[v, level : level + 1], pltpu.roll(c, rows - 1, 0))
            s = jnp.where(row == 0, south_ref[v, level : level + 1], pltpu.roll(c, 1, 0))
            to_ref[v, level] = advance(c, n, s, q_ref[v, up], q_ref[v, low], weight)
        if new_ref is not None:
            sending(level).start()

    for own in range(COLUMNS):

        @pl.when(own_column == own)
        def _():
            for level in range(levs):
                for half in range(2):
                    for k, lane, lanes, lo, hi, column, at, at_lane in field_parts(rows, half):
                        piece_ref = own_ref if column == own else other_ref
                        part = piece_ref[level * 2 + half, at : at + hi - lo].astype(jnp.float32)
                        field_ref[k, lo:hi, lane : lane + lanes] = part[:, at_lane : at_lane + lanes]
                step(level)

    if new_ref is not None:
        for level in range(levs):
            sending(level).wait()


def on_band(kernel, name, outs, out_space, field_rows, flops, args, scratch=()):
    vmem = pl.BlockSpec(memory_space=pltpu.VMEM)
    lon = args[0].shape[-1]
    bytes_accessed = sum(a.size * a.dtype.itemsize for a in (*args, *outs))
    return pl.pallas_call(
        kernel,
        out_shape=outs,
        in_specs=[vmem] * len(args),
        out_specs=tuple(pl.BlockSpec(memory_space=out_space) for _ in outs),
        scratch_shapes=[
            pltpu.VMEM((FIELDS, field_rows, -(-lon // LANES) * LANES), jnp.float32),
            pltpu.VMEM(args[1].shape, jnp.float32),
            pltpu.VMEM(args[1].shape, jnp.float32),
            *scratch,
        ],
        compiler_params=pltpu.CompilerParams(vmem_limit_bytes=VMEM_LIMIT),
        cost_estimate=pl.CostEstimate(flops=flops, bytes_accessed=bytes_accessed, transcendentals=0),
        name=name,
    )(*args)


def edge_rows(*args):
    vecs, levs, _, lon = args[0].shape
    edge = jax.ShapeDtypeStruct((vecs, levs, lon), jnp.float32)
    return on_band(rows_kernel, "edge_rows", (edge, edge), pltpu.VMEM, levs, 30 * edge.size, args)


def one_hour(*args):
    q = args[0]
    out = jax.ShapeDtypeStruct(q.shape, q.dtype)
    return on_band(hour_kernel, "one_hour", (out,), pltpu.VMEM, q.shape[2], 20 * q.size, args)[0]


def last_hour(*args):
    q = args[0]
    out = jax.ShapeDtypeStruct(q.shape, q.dtype)
    scratch = (pltpu.VMEM(q.shape, q.dtype), pltpu.SemaphoreType.DMA((q.shape[1],)))
    return on_band(hour_kernel, "last_hour", (out,), pl.ANY, q.shape[2], 20 * q.size, args, scratch)[0]


def shards(perturb, trajectory, hour_slot, sea_mask):
    lat = lax.axis_size("lat")
    column = this_column()
    odd = odd_band()
    on_chip = [(i, i ^ 1) for i in range(lat)]
    between = [pair for i in range(1, lat - 1, 2) for pair in ((i, i + 1), (i + 1, i))]
    rings = [[c * RING + z for z in range(RING)] for c in range(COLUMNS)]
    swap = [(i, (i + RING) % (COLUMNS * RING)) for i in range(COLUMNS * RING)]

    def halos(to_far, to_near):
        far = lax.ppermute(to_far, "lat", between)
        return far, lax.ppermute(to_near, "lat", on_chip)

    first, last = perturb[:, :, 0], perturb[:, :, -1]
    halo = halos(jnp.where(odd == 1, last, first), jnp.where(odd == 1, first, last))

    end, last_slot = RING - 1, COLUMNS * RING - 1
    keep, send = pack(trajectory)
    crossed = lax.ppermute(send, "vec", swap)
    moved = lax.ppermute(keep, "vec", [(c * RING + end, c * RING + end - 1) for c in range(COLUMNS)])
    asked = hour_slot[0] + hour_slot[1] - last_slot
    both = asked == end
    z = lax.axis_index("vec") % RING
    own_there = jnp.where(z == end, (column == 1) & ~both, asked // RING == column)
    choice = jnp.where((z == end - 1) & both, 2, jnp.where(own_there, 0, 1)).astype(jnp.int32)
    offered = offer(choice[None], keep, crossed, moved)
    place = jnp.where(both & (hour_slot // RING == column), end - 1, hour_slot % RING)

    pieces = lax.all_to_all(offered, "vec", 0, 0, axis_index_groups=rings, tiled=True)
    picked = jnp.stack([lax.dynamic_index_in_dim(pieces, place[h], 0, keepdims=False) for h in range(2)])
    picked = picked + (sum(h[0, 0, 0] for h in halo) * 0).astype(picked.dtype)
    gathered = lax.all_gather(picked, "vec", axis=0, axis_index_groups=rings)
    own = [gathered[:, h] for h in range(2)]
    other = [lax.ppermute(half, "vec", swap) for half in own]

    args = (perturb, *halo, sea_mask, own[0], other[0])
    halo = halos(*edge_rows(*args))
    return last_hour(one_hour(*args), *halo, sea_mask, own[1], other[1])


def solution(mesh):
    return jax.shard_map(
        shards,
        mesh=mesh,
        in_specs=(
            P("vec", None, "lat", None),
            P("vec", None, None, "lat", None),
            P(),
            P("lat", None),
        ),
        out_specs=P("vec", None, "lat", None),
        check_vma=False,
    )
```

```python
import functools

import jax
import jax.numpy as jnp
from jax import lax
from jax.experimental import pallas as pl
from jax.experimental.pallas import tpu as pltpu
from jax.sharding import PartitionSpec as P

COLUMNS = 2
RING = 16
LANES = 128
FIELDS = 3
FULL = 5
TALL = 40
PIECE = 104
VMEM_LIMIT = 48 * 1024 * 1024


def this_column():
    return lax.axis_index("vec") // RING


def odd_band():
    return lax.axis_index("lat") % 2


def level_parts(rows):
    total = FIELDS * rows
    parts = [(t * LANES, LANES, 0, total, t * total, 0) for t in range(FULL)]
    lane, at = FULL * LANES, FULL * total
    parts.append((lane, 64, 0, TALL, at, 0))
    parts.append((lane, 64, TALL, total, at, 64))
    lane, at = lane + 64, at + TALL
    for start in range(0, total, 8):
        down, across = divmod(start // 8, 8)
        parts.append((lane, 16, start, start + 8, at + 8 * down, 16 * across))
    return parts


def field_parts(rows, half):
    parts = []
    for lane, lanes, start, stop, at, at_lane in level_parts(rows):
        for k in range(FIELDS):
            for column in range(COLUMNS):
                top = (half * COLUMNS + column) * PIECE
                lo = max(start, k * rows, start + top - at)
                hi = min(stop, (k + 1) * rows, start + top + PIECE - at)
                if lo < hi:
                    parts.append((k, lane, lanes, lo - k * rows, hi - k * rows, column, at + lo - start - top, at_lane))
    return parts


def pack_kernel(field_ref, keep_ref, send_ref):
    _, levs, rows, lon = field_ref.shape[1:]
    for own in range(COLUMNS):

        @pl.when(this_column() == own)
        def _():
            for level in range(levs):
                for half in range(2):
                    for k, lane, lanes, lo, hi, column, at, at_lane in field_parts(rows, half):
                        piece_ref = keep_ref if column == own else send_ref
                        piece_ref[level * 2 + half, at : at + hi - lo, at_lane : at_lane + lanes] = field_ref[
                            0, k, level, lo:hi, lane : lane + lanes
                        ]


def pack(trajectory):
    half = jax.ShapeDtypeStruct((RING, PIECE, LANES), trajectory.dtype)
    vmem = pl.BlockSpec(memory_space=pltpu.VMEM)
    return pl.pallas_call(
        pack_kernel,
        out_shape=(half, half),
        in_specs=[vmem],
        out_specs=(vmem, vmem),
        compiler_params=pltpu.CompilerParams(vmem_limit_bytes=VMEM_LIMIT),
        name="pack",
    )(trajectory)


def offer_kernel(choice_ref, keep_ref, crossed_ref, moved_ref, offered_ref, done):
    for i, ref in enumerate((keep_ref, crossed_ref, moved_ref)):

        @pl.when(choice_ref[0] == i)
        def _():
            copy = pltpu.make_async_copy(ref, offered_ref, done)
            copy.start()
            copy.wait()


def offer(choice, *halves):
    anywhere = pl.BlockSpec(memory_space=pl.ANY)
    return pl.pallas_call(
        offer_kernel,
        out_shape=jax.ShapeDtypeStruct(halves[0].shape, halves[0].dtype),
        in_specs=[pl.BlockSpec(memory_space=pltpu.SMEM)] + [anywhere] * len(halves),
        out_specs=anywhere,
        scratch_shapes=[pltpu.SemaphoreType.DMA],
        compiler_params=pltpu.CompilerParams(vmem_limit_bytes=VMEM_LIMIT),
        name="offer",
    )(choice, *halves)


def lanes_next(x):
    return jnp.concatenate([x[..., 1:], x[..., :1]], axis=-1)


def lanes_prev(x):
    return jnp.concatenate([x[..., -1:], x[..., :-1]], axis=-1)


def weights(f0, f1, f2, mask):
    diffuse = mask * (0.06 + 0.015 * f0)
    zonal, merid = mask * (0.15 * f1), mask * (0.15 * f2)
    return (
        0.8 * mask - 4.0 * diffuse,
        diffuse - zonal,
        diffuse + zonal,
        diffuse - merid,
        diffuse + merid,
        0.1 * mask,
    )


def advance(c, n, s, u, b, weight):
    wc, we, ww, wn, ws, wl = weight
    return (wc * c + we * lanes_next(c) + ww * lanes_prev(c)) + (wn * n + ws * s + wl * (u + b))


def set_halos(near_ref, far_ref, south_ref, north_ref):
    @pl.when(odd_band() == 1)
    def _():
        south_ref[...] = near_ref[...]
        north_ref[...] = far_ref[...]

    @pl.when(odd_band() == 0)
    def _():
        south_ref[...] = far_ref[...]
        north_ref[...] = near_ref[...]


def row_kernel(
    to_near, q_ref, far_ref, near_ref, mask_ref, own_ref, other_ref,
    row_ref, field_ref, south_ref, north_ref,
):
    vecs, levs, rows, lon = q_ref.shape
    lev = lax.broadcasted_iota(jnp.int32, (levs, lon), 0)
    own_column, odd = this_column(), odd_band()
    set_halos(near_ref, far_ref, south_ref, north_ref)

    def row_of(v, r):
        return jnp.concatenate([q_ref[v, z, r : r + 1] for z in range(levs)], axis=0)

    for r, step in ((0, 1), (rows - 1, -1)):

        @pl.when(odd == (1 if (r == 0) == to_near else 0))
        def _(r=r, step=step):
            for own in range(COLUMNS):

                @pl.when(own_column == own)
                def _():
                    for half in range(2):
                        for k, lane, lanes, lo, hi, column, at, at_lane in field_parts(rows, half):
                            if lo <= r < hi:
                                piece_ref = own_ref if column == own else other_ref
                                base = at + (r - lo) // 8 * 8
                                for z in range(levs):
                                    eight = piece_ref[z * 2 + half, base : base + 8].astype(jnp.float32)
                                    i = (r - lo) % 8
                                    field_ref[k, z : z + 1, lane : lane + lanes] = eight[
                                        i : i + 1, at_lane : at_lane + lanes
                                    ]

            weight = weights(*(field_ref[k, :, :lon] for k in range(FIELDS)), mask_ref[r : r + 1].astype(jnp.float32))
            new = []
            for v in range(vecs):
                c, inner = row_of(v, r), row_of(v, r + step)
                n, s = (inner, south_ref[v]) if r == 0 else (north_ref[v], inner)
                u = jnp.where(lev == 0, c, pltpu.roll(c, 1, 0))
                b = jnp.where(lev == levs - 1, c, pltpu.roll(c, levs - 1, 0))
                new.append(advance(c, n, s, u, b, weight))
            for v in range(vecs):
                row_ref[v] = new[v]


def hour_kernel(
    q_ref, far_ref, near_ref, mask_ref, own_ref, other_ref,
    out_ref, field_ref, south_ref, north_ref, new_ref=None, sent=None,
):
    vecs, levs, rows, lon = q_ref.shape
    row = lax.broadcasted_iota(jnp.int32, (rows, lon), 0)
    mask = mask_ref[...].astype(jnp.float32)
    own_column = this_column()
    set_halos(near_ref, far_ref, south_ref, north_ref)
    to_ref = out_ref if new_ref is None else new_ref

    def sending(level):
        return pltpu.make_async_copy(new_ref.at[:, level], out_ref.at[:, level], sent.at[level])

    def step(level):
        weight = weights(*(field_ref[k, :, :lon] for k in range(FIELDS)), mask)
        up, low = max(level - 1, 0), min(level + 1, levs - 1)
        for v in range(vecs):
            c = q_ref[v, level]
            n = jnp.where(row == rows - 1, north_ref[v, level : level + 1], pltpu.roll(c, rows - 1, 0))
            s = jnp.where(row == 0, south_ref[v, level : level + 1], pltpu.roll(c, 1, 0))
            to_ref[v, level] = advance(c, n, s, q_ref[v, up], q_ref[v, low], weight)
        if new_ref is not None:
            sending(level).start()

    for own in range(COLUMNS):

        @pl.when(own_column == own)
        def _():
            for level in range(levs):
                for half in range(2):
                    for k, lane, lanes, lo, hi, column, at, at_lane in field_parts(rows, half):
                        piece_ref = own_ref if column == own else other_ref
                        part = piece_ref[level * 2 + half, at : at + hi - lo].astype(jnp.float32)
                        field_ref[k, lo:hi, lane : lane + lanes] = part[:, at_lane : at_lane + lanes]
                step(level)

    if new_ref is not None:
        for level in range(levs):
            sending(level).wait()


def on_band(kernel, name, outs, out_space, field_rows, flops, args, scratch=()):
    vmem = pl.BlockSpec(memory_space=pltpu.VMEM)
    lon = args[0].shape[-1]
    bytes_accessed = sum(a.size * a.dtype.itemsize for a in (*args, *outs))
    return pl.pallas_call(
        kernel,
        out_shape=outs,
        in_specs=[vmem] * len(args),
        out_specs=tuple(pl.BlockSpec(memory_space=out_space) for _ in outs),
        scratch_shapes=[
            pltpu.VMEM((FIELDS, field_rows, -(-lon // LANES) * LANES), jnp.float32),
            pltpu.VMEM(args[1].shape, jnp.float32),
            pltpu.VMEM(args[1].shape, jnp.float32),
            *scratch,
        ],
        compiler_params=pltpu.CompilerParams(vmem_limit_bytes=VMEM_LIMIT),
        cost_estimate=pl.CostEstimate(flops=flops, bytes_accessed=bytes_accessed, transcendentals=0),
        name=name,
    )(*args)


def edge_row(to_near, *args):
    vecs, levs, _, lon = args[0].shape
    edge = jax.ShapeDtypeStruct((vecs, levs, lon), jnp.float32)
    name = "near_row" if to_near else "far_row"
    kernel = functools.partial(row_kernel, to_near)
    return on_band(kernel, name, (edge,), pltpu.VMEM, levs, 30 * edge.size, args)[0]


def one_hour(*args):
    q = args[0]
    out = jax.ShapeDtypeStruct(q.shape, q.dtype)
    return on_band(hour_kernel, "one_hour", (out,), pltpu.VMEM, q.shape[2], 20 * q.size, args)[0]


def last_hour(*args):
    q = args[0]
    out = jax.ShapeDtypeStruct(q.shape, q.dtype)
    scratch = (pltpu.VMEM(q.shape, q.dtype), pltpu.SemaphoreType.DMA((q.shape[1],)))
    return on_band(hour_kernel, "last_hour", (out,), pl.ANY, q.shape[2], 20 * q.size, args, scratch)[0]


def shards(perturb, trajectory, hour_slot, sea_mask):
    lat = lax.axis_size("lat")
    column = this_column()
    odd = odd_band()
    on_chip = [(i, i ^ 1) for i in range(lat)]
    between = [pair for i in range(1, lat - 1, 2) for pair in ((i, i + 1), (i + 1, i))]
    rings = [[c * RING + z for z in range(RING)] for c in range(COLUMNS)]
    swap = [(i, (i + RING) % (COLUMNS * RING)) for i in range(COLUMNS * RING)]

    def halos(to_far, to_near):
        far = lax.ppermute(to_far, "lat", between)
        return far, lax.ppermute(to_near, "lat", on_chip)

    first, last = perturb[:, :, 0], perturb[:, :, -1]
    halo = halos(jnp.where(odd == 1, last, first), jnp.where(odd == 1, first, last))

    end, last_slot = RING - 1, COLUMNS * RING - 1
    keep, send = pack(trajectory)
    crossed = lax.ppermute(send, "vec", swap)
    moved = lax.ppermute(keep, "vec", [(c * RING + end, c * RING + end - 1) for c in range(COLUMNS)])
    asked = hour_slot[0] + hour_slot[1] - last_slot
    both = asked == end
    z = lax.axis_index("vec") % RING
    own_there = jnp.where(z == end, (column == 1) & ~both, asked // RING == column)
    choice = jnp.where((z == end - 1) & both, 2, jnp.where(own_there, 0, 1)).astype(jnp.int32)
    offered = offer(choice[None], keep, crossed, moved)
    place = jnp.where(both & (hour_slot // RING == column), end - 1, hour_slot % RING)

    pieces = lax.all_to_all(offered, "vec", 0, 0, axis_index_groups=rings, tiled=True)
    picked = jnp.stack([lax.dynamic_index_in_dim(pieces, place[h], 0, keepdims=False) for h in range(2)])
    picked = picked + (sum(h[0, 0, 0] for h in halo) * 0).astype(picked.dtype)
    gathered = lax.all_gather(picked, "vec", axis=0, axis_index_groups=rings)
    own = [gathered[:, h] for h in range(2)]
    other = [lax.ppermute(half, "vec", swap) for half in own]

    args = (perturb, *halo, sea_mask, own[0], other[0])
    halo = halos(edge_row(False, *args), edge_row(True, *args))
    return last_hour(one_hour(*args), *halo, sea_mask, own[1], other[1])


def solution(mesh):
    return jax.shard_map(
        shards,
        mesh=mesh,
        in_specs=(
            P("vec", None, "lat", None),
            P("vec", None, None, "lat", None),
            P(),
            P("lat", None),
        ),
        out_specs=P("vec", None, "lat", None),
        check_vma=False,
    )
```
